32 devices in a mesh: gx: 4 (over y, core), gy: 8 (over z, x).
Axes of the slice: x: 2, y: 2, z: 4, core: 2. Of those that a mesh axis runs over, the one named last changes fastest.
Arguments:
- rhs: float32 [3, 20, 32, 1024], P(None, None, 'gx', 'gy'), may hold values from -6 to 6
- diag_block: bfloat16 [9, 20, 32, 1024], P(None, None, 'gx', 'gy'), may hold values from -0.5625 to 4.75
- mobility: bfloat16 [9, 20, 32, 1024], P(None, None, 'gx', 'gy'), may hold values from -0.34375 to 1.375
- trans: bfloat16 [3, 20, 32, 1024], P(None, None, 'gx', 'gy'), may hold values from 0.5 to 1
- perf_cell: int32 [32, 8, 32], P(('gx', 'gy')), may hold values from 0 to 20479, as said below
- perf_pi: float32 [32, 8, 32], P(('gx', 'gy')), may hold values from 0 to 0.6, as said below
- perf_seg: int32 [32, 8, 32], P(('gx', 'gy')), may hold values from 0 to 255
- seg_parent: int32 [8192], P(('gx', 'gy')), may hold values from -1 to 254, as said below
- seg_trans: float32 [8192], P(('gx', 'gy')), may hold values from 0.5 to 2
- seg_rhs: float32 [8192], P(('gx', 'gy')), may hold values from -6 to 6
Outputs:
- solution: float32 [3, 20, 32, 1024], P(None, None, 'gx', 'gy')
- seg_pressure: float32 [8192], P(('gx', 'gy'))
The draws below stay inside these ranges and needn't reach their ends.
Inputs may be any that keep to these rules, and one draw needn't show every extreme that they name: `perf_cell`: the 8 slots of a sender-owner pair name consecutive cells along y in one layer and one x column. `perf_pi`: live slots of a sender-owner pair come first among its 8; every sender has one owner with all 8 slots live, and one owner receives all 8 from every sender; some of the owners, drawn from the seed, receive many more than the rest. `seg_parent`: A parent comes just before its segment on the same owner; segment 0 of every owner is at a well head.
All inputs are finite; a program needn't handle non-finite values.
Results may differ from the reference program's by a relative error of at most 0.0003.
Values may be sent and summed in bfloat16 or wider, within the bound.
A program may use at most 128 MiB of HBM per device.

```python
import math
import jax
import jax.numpy as jnp

COMP = 3
CX = 8
CY = 128
NZ = 20
CAP = 8
SEG_DEV = 256
SWEEPS = 4
OUTER = 2
OWNERS = 32
NX = 32
NY = 1024
SEGS = 8192
N_GY = 8


def draw_rhs(key, part):
    shape = (COMP, NZ, NX, NY)
    base = jax.random.truncated_normal(jax.random.fold_in(key, 7), -6.0, 6.0, shape, jnp.float32)
    return base


def draw_diag_block(key, part):
    first, second = jax.random.split(key)
    shape = (COMP * COMP, NZ, NX, NY)
    ondiag = jax.random.uniform(first, shape, jnp.float32, 3.25, 4.75)
    offdiag = jax.random.uniform(second, shape, jnp.float32, -0.375, 0.375)
    place = (jnp.arange(COMP * COMP) % 4 == 0)[:, None, None, None]
    return jnp.where(place, ondiag, offdiag).astype(jnp.bfloat16)


def draw_mobility(key, part):
    first, second = jax.random.split(jax.random.fold_in(key, 5))
    shape = (COMP * COMP, NZ, NX, NY)
    ondiag = jax.random.uniform(first, shape, jnp.float32, 0.6875, 1.375)
    offdiag = jax.random.uniform(second, shape, jnp.float32, -0.25, 0.25)
    place = (jnp.arange(COMP * COMP) % 4 == 0)[:, None, None, None]
    return jnp.where(place, ondiag, offdiag).astype(jnp.bfloat16)


def draw_perf_cell(key, part):
    keys = jax.random.split(jax.random.fold_in(key, 11), 3)
    layer = jax.random.randint(keys[0], (OWNERS, 1, OWNERS), 0, NZ)
    column = jax.random.randint(keys[1], (OWNERS, 1, OWNERS), 0, CX)
    start = jax.random.randint(keys[2], (OWNERS, 1, OWNERS), 0, CY - CAP + 1)
    sender = jnp.arange(OWNERS)[:, None, None]
    owner = jnp.arange(OWNERS)[None, None, :]
    last_pair = (sender == 0) & (owner == 0)
    first_pair = (sender == 0) & (owner == 1)
    layer = jnp.where(last_pair, NZ - 1, jnp.where(first_pair, 0, layer))
    column = jnp.where(last_pair, CX - 1, jnp.where(first_pair, 0, column))
    start = jnp.where(last_pair, CY - CAP, jnp.where(first_pair, 0, start))
    steps_along = jnp.arange(CAP)[None, :, None]
    return (layer * (CX * CY) + column * CY + start + steps_along).astype(jnp.int32)


def draw_perf_pi(key, part):
    keys = jax.random.split(jax.random.fold_in(key, 3), 6)
    heavy = jax.random.randint(keys[0], (OWNERS,), 0, 4) == 0
    light = jax.random.randint(keys[1], (OWNERS, OWNERS), 0, CAP // 4 + 1)
    loaded = jax.random.randint(keys[2], (OWNERS, OWNERS), CAP // 2, CAP + 1)
    count = jnp.where(heavy[None, :], loaded, light)
    offset = jax.random.randint(keys[3], (), 0, OWNERS)
    target = jax.random.randint(keys[4], (), 0, OWNERS)
    sender = jnp.arange(OWNERS)[:, None]
    owner = jnp.arange(OWNERS)[None, :]
    full = (owner == (sender + offset) % OWNERS) | (owner == target)
    count = jnp.where(full, CAP, count)
    live = jnp.arange(CAP)[None, :, None] < count[:, None, :]
    values = jnp.exp(jax.random.uniform(keys[5], (OWNERS, CAP, OWNERS), jnp.float32, jnp.log(0.1), jnp.log(0.6)))
    return jnp.where(live, values, 0.0)


def draw_seg_parent(key, part):
    flags = jax.random.randint(jax.random.fold_in(key, 9), (SEGS,), 0, 6)
    local = jnp.arange(SEGS, dtype=jnp.int32) % SEG_DEV
    head = (flags == 0) & (local != SEG_DEV - 1) | (local == 0)
    return jnp.where(head, -1, local - 1).astype(jnp.int32)


def touch_ends(values, key, low, high):
    longest = values.shape.index(max(values.shape))
    spots = []
    for shift in (0, 1):
        where = [jax.random.randint(jax.random.fold_in(key, axis), (), 0, length) for axis, length in enumerate(values.shape)]
        where[longest] = (where[longest] + shift) % values.shape[longest]
        spots.append(tuple(where))
    return values.at[spots[0]].set(low).at[spots[1]].set(high)


def block_scale(stream_key, dims, shards, smallest, high):
    gain = 1.0
    for dim, parts in shards:
        draws = jax.random.uniform(jax.random.fold_in(jax.random.fold_in(stream_key, 6), dim), (parts,), jnp.float32, smallest / len(shards), high / len(shards))
        gain = gain * jnp.repeat(jnp.exp(draws), dims[dim] // parts).reshape((-1,) + (1,) * (len(dims) - 1 - dim))
    return gain


def bell_draw(stream_key, dims, width, reach, cuts=(), kind=jnp.bfloat16):
    array = jax.random.normal(stream_key, dims, jnp.float32) * width
    if len(cuts) > 0:
        array = block_scale(stream_key, dims, cuts, -0.22, 0.18) * array
    return jnp.clip(array, min=-reach, max=reach).astype(kind)


def setup_inputs(seed: int = 0) -> dict:
    streams_of = jax.random.split(jax.random.key(seed), 11)
    return {
        "rhs": draw_rhs(jax.random.fold_in(streams_of[10], 71), 0),
        "diag_block": draw_diag_block(jax.random.fold_in(streams_of[10], 71), 0),
        "mobility": draw_mobility(jax.random.fold_in(streams_of[10], 71), 0),
        "trans": jnp.clip(jnp.exp(math.log(1.0) - 0.6931472 * jax.random.uniform(streams_of[3], (COMP, NZ, NX, NY), jnp.float32) ** block_scale(streams_of[3], (COMP, NZ, NX, NY), ((2, 4), (3, 8)), -0.2, 0.2)), 0.5, 1.0).astype(jnp.bfloat16),
        "perf_cell": draw_perf_cell(jax.random.fold_in(streams_of[10], 71), 0),
        "perf_pi": draw_perf_pi(jax.random.fold_in(streams_of[10], 71), 0),
        "perf_seg": touch_ends(jax.random.randint(streams_of[6], (OWNERS, CAP, OWNERS), 0, SEG_DEV), jax.random.fold_in(streams_of[6], 1), 0, SEG_DEV - 1).astype(jnp.int32),
        "seg_parent": draw_seg_parent(jax.random.fold_in(streams_of[10], 71), 0),
        "seg_trans": jnp.clip(jnp.exp(math.log(2.0) - 1.3862944 * jax.random.uniform(streams_of[8], (SEGS,), jnp.float32) ** block_scale(streams_of[8], (SEGS,), ((0, 32),), -0.2, 0.2)), 0.5, 2.0),
        "seg_rhs": bell_draw(streams_of[9], (SEGS,), 1.0, 6.0, ((0, 32),), jnp.float32),
    }


def invert_blocks(mat):
    a, b, c, d, e, f, g, h, i = [mat[position] for position in range(9)]
    first = e * i - f * h
    second = f * g - d * i
    third = d * h - e * g
    determinant = a * first + b * second + c * third
    entries = [first, c * h - b * i, b * f - c * e, second, a * i - c * g, c * d - a * f, third, b * g - a * h, a * e - b * d]
    return jnp.stack([entry / determinant for entry in entries])


def block_apply(mat, vec):
    return jnp.stack([mat[3 * row] * vec[0] + mat[3 * row + 1] * vec[1] + mat[3 * row + 2] * vec[2] for row in range(3)])


def reference(rhs, diag_block, mobility, trans, perf_cell, perf_pi, perf_seg, seg_parent, seg_trans, seg_rhs):
    dense = diag_block.astype(jnp.float32)
    mob_full = mobility.astype(jnp.float32)
    trans_f = trans.astype(jnp.float32)
    inverse = invert_blocks(dense)
    face_x = trans_f[0, :, :-1, :] * trans_f[0, :, 1:, :]
    face_y = trans_f[1, :, :, :-1] * trans_f[1, :, :, 1:]
    face_z = trans_f[2, :-1] * trans_f[2, 1:]
    sender = jnp.arange(OWNERS, dtype=jnp.int32)[:, None, None]
    owner = jnp.arange(OWNERS, dtype=jnp.int32)[None, None, :]
    layer = perf_cell // (CX * CY)
    column_x = (sender // N_GY) * CX + (perf_cell // CY) % CX
    column_y = (sender % N_GY) * CY + perf_cell % CY
    cell_flat = (layer * (NX * NY) + column_x * NY + column_y).reshape(-1).astype(jnp.int32)
    seg_flat = (owner * SEG_DEV + jnp.transpose(perf_seg, (2, 1, 0))).reshape(-1).astype(jnp.int32)
    weights = perf_pi.reshape(-1)
    parent = seg_parent.reshape(OWNERS, SEG_DEV)
    seg_tw = seg_trans.reshape(OWNERS, SEG_DEV)

    def child_total(values):
        def one_owner(vals, par):
            return jax.ops.segment_sum(jnp.where(par >= 0, vals, 0.0), jnp.maximum(par, 0), num_segments=SEG_DEV)
        return jax.vmap(one_owner)(values, parent)

    pi_sum = jnp.zeros((SEGS,), jnp.float32).at[seg_flat].add(weights)
    seg_diag = (seg_tw + child_total(seg_tw)).reshape(-1) + pi_sum

    def residuals(field, seg_state):
        mob_vec = block_apply(mob_full, field)
        near = jnp.zeros_like(field)
        near = near.at[:, :, :-1, :].add(face_x * mob_vec[:, :, 1:, :])
        near = near.at[:, :, 1:, :].add(face_x * mob_vec[:, :, :-1, :])
        near = near.at[:, :, :, :-1].add(face_y * mob_vec[:, :, :, 1:])
        near = near.at[:, :, :, 1:].add(face_y * mob_vec[:, :, :, :-1])
        near = near.at[:, :-1].add(face_z * mob_vec[:, 1:])
        near = near.at[:, 1:].add(face_z * mob_vec[:, :-1])
        flows = weights * (field[0].reshape(-1)[cell_flat] - seg_state[seg_flat])
        into_cells = jnp.zeros((NZ * NX * NY,), jnp.float32).at[cell_flat].add(flows).reshape(NZ, NX, NY)
        cell_res = rhs - block_apply(dense, field) + near - mob_full[0::3] * into_cells
        state = seg_state.reshape(OWNERS, SEG_DEV)
        above = jnp.where(parent >= 0, jnp.take_along_axis(state, jnp.maximum(parent, 0), axis=1), 0.0)
        flux = seg_tw * (state - above)
        into_segs = jnp.zeros((SEGS,), jnp.float32).at[seg_flat].add(flows)
        seg_res = seg_rhs - flux.reshape(-1) + child_total(flux).reshape(-1) + into_segs
        return cell_res, seg_res

    solution = jnp.zeros_like(rhs)
    seg_pressure = jnp.zeros_like(seg_rhs)
    cell_res, seg_res = rhs, seg_rhs
    for outer in range(OUTER):
        field, seg_state = solution, seg_pressure
        cell_now, seg_now = cell_res, seg_res
        for sweep in range(SWEEPS):
            field = field + block_apply(inverse, cell_now)
            seg_state = seg_state + seg_now / seg_diag
            cell_now, seg_now = residuals(field, seg_state)
        cell_diff = cell_res - cell_now
        seg_diff = seg_res - seg_now
        numer = jnp.sum(cell_res * cell_diff) + jnp.sum(seg_res * seg_diff)
        denom = jnp.sum(cell_diff * cell_diff) + jnp.sum(seg_diff * seg_diff)
        omega = numer / denom
        solution = solution + omega * (field - solution)
        seg_pressure = seg_pressure + omega * (seg_state - seg_pressure)
        cell_res = cell_res - omega * cell_diff
        seg_res = seg_res - omega * seg_diff
    return solution, seg_pressure
```

```python
import functools

import jax
import jax.numpy as jnp
from jax import lax
from jax.experimental import pallas as pl
from jax.experimental.pallas import tpu as pltpu
from jax.sharding import PartitionSpec as P

SWEEPS = 4
SUB, LANE = 8, 128
SLOTS = 8
MESH = pl.DeviceIdType.MESH
F32 = jnp.float32


def apply3(mat, vec):
    return [mat[3 * r] * vec[0] + mat[3 * r + 1] * vec[1] + mat[3 * r + 2] * vec[2] for r in range(3)]


def inverse3(m):
    a, b, c, d, e, f, g, h, i = m
    first = e * i - f * h
    second = f * g - d * i
    third = d * h - e * g
    inv = 1.0 / (a * first + b * second + c * third)
    entries = [
        first, c * h - b * i, b * f - c * e,
        second, a * i - c * g, c * d - a * f,
        third, b * g - a * h, a * e - b * d,
    ]
    return [entry * inv for entry in entries]


def kernel(
    nx, ny, layers, seg_rows,
    rhs, diag, mob, trans, cell_s, cell_v, perf_pi, perf_seg, parent, seg_trans, seg_rhs,
    out_u, out_w,
    v, tx, ty, tz, part, res, v4, a4, dinv, dd, mm, tt, ty_edge, into,
    onehot, feed, pi_row, k_of, idx, rows, send, recv, ypack, yrecv, xrecv,
    turn_i, turn_f, seg, sums,
    halo_send, halo_recv, msg_send, msg_recv,
):
    n = nx * ny
    my_x, my_y = lax.axis_index("gx"), lax.axis_index("gy")
    me = my_x * ny + my_y
    barrier = pltpu.get_barrier_semaphore()

    def partner(j):
        pos = lax.rem(me + j, n)
        return (lax.div(pos, ny), lax.rem(pos, ny))

    def greet(j, carry):
        pl.semaphore_signal(barrier, inc=1, device_id=partner(j), device_id_type=MESH)
        return carry

    xrecv[...] = jnp.zeros_like(xrecv)
    yrecv[...] = jnp.zeros_like(yrecv)
    lax.fori_loop(1, n, greet, 0)

    has_x = [my_x > 0, my_x < nx - 1]
    has_y = [my_y > 0, my_y < ny - 1]

    def halos(slot):
        below_x, above_x = lax.max(my_x - 1, 0), lax.min(my_x + 1, nx - 1)
        below_y, above_y = lax.max(my_y - 1, 0), lax.min(my_y + 1, ny - 1)

        def copy(src, dst, way, device):
            return pltpu.make_async_remote_copy(
                src_ref=src, dst_ref=dst, send_sem=halo_send.at[slot, way],
                recv_sem=halo_recv.at[slot, way], device_id=device, device_id_type=MESH,
            )

        return [
            (has_x[1], has_x[0], copy(
                tx.at[:, :, SUB - 1:SUB, :], xrecv.at[slot, :, :, 0:1, :], 0, (above_x, my_y))),
            (has_x[0], has_x[1], copy(
                tx.at[:, :, 0:1, :], xrecv.at[slot, :, :, SUB - 1:SUB, :], 1, (below_x, my_y))),
            (has_y[1], has_y[0], copy(ypack.at[slot], yrecv.at[slot, 0], 2, (my_x, above_y))),
            (has_y[0], has_y[1], copy(ypack.at[slot], yrecv.at[slot, 1], 3, (my_x, below_y))),
        ]

    def send_halos(slot):
        for to, _, copy in halos(slot):
            pl.when(to)(copy.start)

    def wait_halos(slot):
        for to, come, copy in halos(slot):
            pl.when(come)(copy.wait_recv)
            pl.when(to)(copy.wait_send)

    def send_rows(slot):
        def one(j, carry):
            target = partner(j)
            pos = target[0] * ny + target[1]
            pltpu.make_async_remote_copy(
                src_ref=send.at[slot, pl.ds(pos, 1), :], dst_ref=recv.at[slot, pl.ds(me, 1), :],
                send_sem=msg_send.at[slot], recv_sem=msg_recv.at[slot],
                device_id=target, device_id_type=MESH,
            ).start()
            return carry

        lax.fori_loop(1, n, one, 0)

    def wait_rows(slot):
        some = pl.ds(0, n - 1)
        copy = pltpu.make_async_remote_copy(
            src_ref=send.at[slot, some, :], dst_ref=recv.at[slot, some, :],
            send_sem=msg_send.at[slot], recv_sem=msg_recv.at[slot],
            device_id=(my_x, my_y), device_id_type=MESH,
        )
        copy.wait_recv()
        copy.wait_send()

    row_n = lax.broadcasted_iota(jnp.int32, (n, LANE), 0)
    lane_n = lax.broadcasted_iota(jnp.int32, (n, LANE), 1)

    def arrived(slot):
        return jnp.where(row_n == me, send[slot], recv[slot])

    turn_i[...] = jnp.zeros_like(turn_i)
    turn_f[...] = jnp.zeros_like(turn_f)
    turn_i[0:SLOTS, 0:n] = cell_v[0]
    turn_i[SLOTS:2 * SLOTS, 0:n] = perf_seg[0]
    turn_f[0:SLOTS, 0:n] = perf_pi[0]
    places = turn_i[...].T[0:n, :]
    weights = turn_f[...].T[0:n, :]
    send[0] = weights
    pl.semaphore_wait(barrier, n - 1)
    send_rows(0)

    lanes_at = lax.rem(places, LANE)
    idx[...] = lanes_at
    spread = jnp.zeros((n, LANE), F32)
    slot_of = jnp.zeros((n, LANE), jnp.int32)
    for k in range(SLOTS):
        here = lane_n == lanes_at[:, k:k + 1]
        spread = spread + jnp.where(here, weights[:, k:k + 1], 0.0)
        slot_of = jnp.where(here, SLOTS + k, slot_of)
    pi_row[...] = spread
    k_of[...] = slot_of
    row_id = lax.div(cell_v[0][0:1, :], LANE)
    grid_rows = lax.broadcasted_iota(jnp.int32, (layers * SUB, n), 0)
    onehot[...] = jnp.where(grid_rows == row_id, 1.0, 0.0).astype(jnp.bfloat16)

    def scatter(field):
        table = onehot[...]
        high = field.astype(jnp.bfloat16)
        rest = field - high.astype(F32)
        mid = rest.astype(jnp.bfloat16)
        low = (rest - mid.astype(F32)).astype(jnp.bfloat16)
        total = jnp.dot(table, low, preferred_element_type=F32)
        total = total + jnp.dot(table, mid, preferred_element_type=F32)
        return total + jnp.dot(table, high, preferred_element_type=F32)

    into[...] = scatter(spread).reshape(layers, SUB, LANE)

    zc = 4 if layers % 4 == 0 else 1
    chunks = [slice(z, z + zc) for z in range(0, layers, zc)]
    lane = lax.broadcasted_iota(jnp.int32, (SUB, LANE), 1)
    row = lax.broadcasted_iota(jnp.int32, (SUB, LANE), 0)
    edge = (lane == 0) | (lane == LANE - 1)

    tz[:, 0] = jnp.zeros((3, SUB, LANE), F32)
    tz[:, layers + 1] = jnp.zeros((3, SUB, LANE), F32)

    def flat(zs):
        return slice(zs.start * SUB, zs.stop * SUB)

    def publish(zs, vec, packed):
        mv = apply3([mm[i, zs] for i in range(9)], vec)
        for c in range(3):
            v[c, flat(zs), :] = vec[c].reshape(zc * SUB, LANE)
            tx[c, zs] = tt[0, zs] * mv[c]
            along = tt[1, zs] * mv[c]
            ty[c, zs] = along
            tz[c, zs.start + 1:zs.stop + 1] = tt[2, zs] * mv[c]
            for z in range(zs.start, zs.stop):
                shift = (2 * (c * layers + z)) % LANE
                moved = along[z - zs.start]
                if shift:
                    moved = pltpu.roll(moved, shift, 1)
                mine = (lane == (shift - 1) % LANE) | (lane == shift)
                packed = jnp.where(mine, moved, packed)
        return packed

    packed = jnp.zeros((SUB, LANE), F32)
    for zs in chunks:
        dense = [diag[i, zs].astype(F32) for i in range(9)]
        mobile = [mob[i, zs].astype(F32) for i in range(9)]
        inv = inverse3(dense)
        perf = into[zs]
        for i in range(9):
            dinv[i, zs] = inv[i]
            mm[i, zs] = mobile[i]
            dd[i, zs] = dense[i] + mobile[i] * perf if i % 3 == 0 else dense[i]
        for i in range(3):
            tt[i, zs] = trans[i, zs].astype(F32)
        ty_edge[zs] = jnp.where(edge, tt[1, zs], 0.0)
        packed = publish(zs, apply3(inv, [rhs[c, zs] for c in range(3)]), packed)
    ypack[1] = packed

    seg[...] = jnp.zeros_like(seg)
    seg[0, 0:seg_rows, :] = jnp.where(parent[...] >= 0, seg_trans[...], 0.0)
    seg[2, 0:seg_rows, :] = seg_trans[...]
    seg[3, 0:seg_rows, :] = seg_rhs[...]

    def before(x):
        moved = pltpu.roll(x, 1, 1)
        return jnp.where(lane == 0, pltpu.roll(moved, 1, 0), moved)

    def after(x):
        moved = pltpu.roll(x, LANE - 1, 1)
        return jnp.where(lane == LANE - 1, pltpu.roll(moved, SUB - 1, 0), moved)

    def tile(parts):
        total = jnp.zeros((SUB, LANE), F32)
        for r in range(seg_rows):
            total = jnp.where(row == r, jnp.sum(parts[r], axis=0, keepdims=True), total)
        return total

    seg[1] = after(seg[0])
    wait_rows(0)
    came = arrived(0)
    parts = [jnp.zeros((n, LANE), F32) for _ in range(seg_rows)]
    for k in range(SLOTS):
        goes = places[:, SLOTS + k:SLOTS + k + 1]
        for r in range(seg_rows):
            term = jnp.where(lane_n + r * LANE == goes, came[:, k:k + 1], 0.0)
            feed[k, r] = term
            parts[r] = parts[r] + term
    turn_i[0:n, :] = lax.div(places, LANE)
    seg[2] = jnp.where(row < seg_rows, seg[2] + seg[1] + tile(parts), 1.0)
    seg[4] = seg[3] / seg[2]
    sums[...] = jnp.zeros_like(sums)

    def fill(slot):
        for o in range(n):
            at = lax.div(cell_s[0, 0, o], LANE)
            rows[o:o + 1, :] = v[0, pl.ds(at, 1), :]
        where_to = idx[...]
        which = turn_i[0:n, :]
        state = seg[4]
        row_vals = jnp.take_along_axis(rows[...], where_to, axis=1, mode="promise_in_bounds")
        seg_vals = jnp.zeros((n, LANE), F32)
        for r in range(seg_rows):
            whole = jnp.broadcast_to(state[r:r + 1, :], (n, LANE))
            got = jnp.take_along_axis(whole, where_to, axis=1, mode="promise_in_bounds")
            seg_vals = jnp.where(which == r, got, seg_vals)
        total = jnp.broadcast_to(sums[0:1, :], (n, LANE))
        send[slot] = jnp.where(
            lane_n < SLOTS, row_vals, jnp.where(lane_n < 2 * SLOTS, seg_vals, total))

    fill(1)

    def inside():
        for zs in chunks:
            vec = [v[c, flat(zs), :].reshape(zc, SUB, LANE) for c in range(3)]
            pulled = apply3([dd[i, zs] for i in range(9)], vec)
            for c in range(3):
                x, y = tx[c, zs], ty[c, zs]
                near_x = (
                    jnp.where(row == 0, 0.0, pltpu.roll(x, 1, 1))
                    + jnp.where(row == SUB - 1, 0.0, pltpu.roll(x, SUB - 1, 1)))
                near_y = (
                    jnp.where(lane == 0, 0.0, pltpu.roll(y, 1, 2))
                    + jnp.where(lane == LANE - 1, 0.0, pltpu.roll(y, LANE - 1, 2)))
                near_z = tz[c, zs] + tz[c, zs.start + 2:zs.stop + 2]
                part[c, zs] = (
                    rhs[c, zs] - pulled[c]
                    + (tt[0, zs] * near_x + tt[1, zs] * near_y + tt[2, zs] * near_z))

    def segments(came):
        parts = [jnp.zeros((n, LANE), F32) for _ in range(seg_rows)]
        for k in range(SLOTS):
            value = jnp.broadcast_to(came[:, k:k + 1], (n, LANE))
            for r in range(seg_rows):
                parts[r] = parts[r] + value * feed[k, r]
        g = seg[4]
        return (
            seg[3] - seg[2] * g + seg[0] * before(g) + seg[1] * after(g) + tile(parts))

    def receive(slot):
        wait_rows(slot)
        came = arrived(slot)
        pressure = jnp.take_along_axis(came, k_of[...], axis=1, mode="promise_in_bounds")
        into[...] = scatter(pi_row[...] * pressure).reshape(layers, SUB, LANE)
        seg[5] = segments(came)
        wait_halos(slot)
        border = jnp.where(
            lax.rem(lane, 2) == 0,
            pltpu.roll(yrecv[slot, 0], 1, 1), pltpu.roll(yrecv[slot, 1], LANE - 1, 1))
        return came, border

    def residual(zs, slot, border):
        vec = []
        for c in range(3):
            total = part[c, zs] + tt[0, zs] * xrecv[slot, c, zs] + mm[3 * c, zs] * into[zs]
            sides = []
            for z in range(zs.start, zs.stop):
                shift = (2 * (c * layers + z)) % LANE
                sides.append(pltpu.roll(border, LANE - shift, 1) if shift else border)
            total = total + ty_edge[zs] * jnp.stack(sides)
            res[c, zs] = total
            vec.append(total)
        return vec

    def put_sums(numer, denom):
        first = jnp.sum(jnp.sum(numer, axis=0, keepdims=True), axis=1, keepdims=True)
        second = jnp.sum(jnp.sum(denom, axis=0, keepdims=True), axis=1, keepdims=True)
        sums[...] = jnp.where(
            lane == 2 * SLOTS, first, jnp.where(lane == 2 * SLOTS + 1, second, 0.0))

    def ratio(came):
        total = jnp.sum(came, axis=0, keepdims=True)
        return total[:, 2 * SLOTS:2 * SLOTS + 1] / total[:, 2 * SLOTS + 1:2 * SLOTS + 2]

    def keep_state():
        for c in range(3):
            for zs in chunks:
                v4[c, zs] = v[c, flat(zs), :].reshape(zc, SUB, LANE)
        seg[6] = seg[4]

    def keep_residual():
        numer = seg[3] * (seg[3] - seg[5])
        denom = (seg[3] - seg[5]) * (seg[3] - seg[5])
        seg[7] = seg[5]
        for c in range(3):
            for zs in chunks:
                last, start = res[c, zs], rhs[c, zs]
                a4[c, zs] = last
                diff = start - last
                numer = numer + jnp.sum(start * diff, axis=0)
                denom = denom + jnp.sum(diff * diff, axis=0)
        put_sums(numer, denom)

    def exchange(k, slot):
        send_rows(slot)
        send_halos(slot)
        inside()
        pl.when(k == SWEEPS)(keep_state)
        pl.when(k == SWEEPS + 1)(keep_residual)

    def sweep(k, carry):
        slot = lax.rem(k, 2)
        exchange(k, slot)
        came, border = receive(slot)

        @pl.when(k == SWEEPS + 2)
        def _():
            sums[1:2, :] = jnp.broadcast_to(ratio(came), (1, LANE))

        seg[4] = seg[4] + seg[5] / seg[2]
        packed = jnp.zeros((SUB, LANE), F32)
        for zs in chunks:
            step = apply3([dinv[i, zs] for i in range(9)], residual(zs, slot, border))
            vec = [v[c, flat(zs), :].reshape(zc, SUB, LANE) + step[c] for c in range(3)]
            packed = publish(zs, vec, packed)
        ypack[1 - slot] = packed
        fill(1 - slot)
        return carry

    last = 2 * SWEEPS
    lax.fori_loop(1, last, sweep, 0)
    slot = last % 2
    omega = sums[1:2, :]
    exchange(last, slot)
    _, border = receive(slot)

    def mix(old, new):
        return old + omega * (new - old)

    start, middle, end = seg[3], seg[7], seg[5]
    first = mix(start, middle)
    diff = first - mix(middle, end)
    numer, denom = first * diff, diff * diff
    for zs in chunks:
        now = residual(zs, slot, border)
        for c in range(3):
            middle = a4[c, zs]
            first = mix(rhs[c, zs], middle)
            diff = first - mix(middle, now[c])
            numer = numer + jnp.sum(first * diff, axis=0)
            denom = denom + jnp.sum(diff * diff, axis=0)
    put_sums(numer, denom)
    send[1] = jnp.broadcast_to(sums[0:1, :], (n, LANE))
    send_rows(1)
    wait_rows(1)
    second = jnp.broadcast_to(ratio(arrived(1)), (1, LANE))

    def combine(middle, end):
        base = omega * middle
        return base + second * (mix(middle, end) - base)

    for c in range(3):
        for zs in chunks:
            out_u[c, zs] = combine(v4[c, zs], v[c, flat(zs), :].reshape(zc, SUB, LANE))
    out_w[...] = combine(seg[6], seg[4])[0:seg_rows, :]


def on_device(
    rhs, diag_block, mobility, trans, perf_cell, perf_pi, perf_seg, seg_parent, seg_trans, seg_rhs
):
    nx, ny = lax.axis_size("gx"), lax.axis_size("gy")
    n = nx * ny
    layers = rhs.shape[1]
    seg_rows = seg_rhs.shape[0] // LANE
    tiles = (seg_rows, LANE)
    cells = (layers, SUB, LANE)
    vmem = pl.BlockSpec(memory_space=pltpu.VMEM)
    scratch = lambda *shape: pltpu.VMEM(shape, F32)
    u, w = pl.pallas_call(
        functools.partial(kernel, nx, ny, layers, seg_rows),
        out_shape=[
            jax.ShapeDtypeStruct(rhs.shape, F32), jax.ShapeDtypeStruct(tiles, F32)],
        in_specs=[vmem] * 4 + [pl.BlockSpec(memory_space=pltpu.SMEM)] + [vmem] * 6,
        out_specs=[vmem] * 2,
        scratch_shapes=[
            scratch(3, layers * SUB, LANE), scratch(3, *cells), scratch(3, *cells),
            scratch(3, layers + 2, SUB, LANE), scratch(3, *cells), scratch(3, *cells),
            scratch(3, *cells), scratch(3, *cells), scratch(9, *cells), scratch(9, *cells),
            scratch(9, *cells), scratch(3, *cells), scratch(*cells), scratch(*cells),
            pltpu.VMEM((layers * SUB, n), jnp.bfloat16),
            scratch(SLOTS, seg_rows, n, LANE), scratch(n, LANE),
            pltpu.VMEM((n, LANE), jnp.int32), pltpu.VMEM((n, LANE), jnp.int32),
            scratch(n, LANE), scratch(2, n, LANE), scratch(2, n, LANE),
            scratch(2, SUB, LANE), scratch(2, 2, SUB, LANE), scratch(2, 3, *cells),
            pltpu.VMEM((LANE, LANE), jnp.int32), scratch(LANE, LANE),
            scratch(8, SUB, LANE), scratch(SUB, LANE),
            pltpu.SemaphoreType.DMA((2, 4)), pltpu.SemaphoreType.DMA((2, 4)),
            pltpu.SemaphoreType.DMA((2,)), pltpu.SemaphoreType.DMA((2,)),
        ],
        compiler_params=pltpu.CompilerParams(
            collective_id=0, has_side_effects=True, vmem_limit_bytes=40 * 1024 * 1024),
        name="sweeps",
    )(
        rhs, diag_block, mobility, trans, perf_cell, perf_cell, perf_pi, perf_seg,
        seg_parent.reshape(tiles), seg_trans.reshape(tiles), seg_rhs.reshape(tiles),
    )
    return u, w.reshape(-1)


def solution(mesh):
    return jax.shard_map(
        on_device,
        mesh=mesh,
        in_specs=(
            P(None, None, "gx", "gy"),
            P(None, None, "gx", "gy"),
            P(None, None, "gx", "gy"),
            P(None, None, "gx", "gy"),
            P(("gx", "gy"), None, None),
            P(("gx", "gy"), None, None),
            P(("gx", "gy"), None, None),
            P(("gx", "gy")),
            P(("gx", "gy")),
            P(("gx", "gy")),
        ),
        out_specs=(P(None, None, "gx", "gy"), P(("gx", "gy"))),
        check_vma=False,
    )
```

```python
import functools

import jax
import jax.numpy as jnp
from jax import lax
from jax.experimental import pallas as pl
from jax.experimental.pallas import tpu as pltpu
from jax.sharding import PartitionSpec as P

SWEEPS = 4
SUB, LANE = 8, 128
SLOTS = 8
MESH = pl.DeviceIdType.MESH
F32 = jnp.float32


def apply3(mat, vec):
    return [mat[3 * r] * vec[0] + mat[3 * r + 1] * vec[1] + mat[3 * r + 2] * vec[2] for r in range(3)]


def inverse3(m):
    a, b, c, d, e, f, g, h, i = m
    first = e * i - f * h
    second = f * g - d * i
    third = d * h - e * g
    inv = 1.0 / (a * first + b * second + c * third)
    entries = [
        first, c * h - b * i, b * f - c * e,
        second, a * i - c * g, c * d - a * f,
        third, b * g - a * h, a * e - b * d,
    ]
    return [entry * inv for entry in entries]


def kernel(
    nx, ny, layers, seg_rows,
    rhs_h, diag_h, mob_h, trans_h, cell_h, pi_h, seg_h, parent_h, seg_trans_h, seg_rhs_h,
    out_u, out_w,
    rhs, diag, mob, trans, cell_s, cell_v, perf_pi, perf_seg, parent, seg_trans, seg_rhs,
    v, tx, ty, tz, part, res, v4, a4, dinv, dd, mm, kk, tt, ty_edge, into,
    onehot, same, feed, pi_row, k_of, idx, rows, k_rows, flow, send, recv, ypack, yrecv, xrecv,
    turn_i, turn_f, seg, sums,
    halo_send, halo_recv, msg_send, msg_recv, load_sem,
):
    n = nx * ny
    my_x, my_y = lax.axis_index("gx"), lax.axis_index("gy")
    me = my_x * ny + my_y
    barrier = pltpu.get_barrier_semaphore()

    loads = [
        pltpu.make_async_copy(src, dst, load_sem.at[i])
        for i, (src, dst) in enumerate([
            (cell_h, cell_v), (pi_h, perf_pi), (seg_h, perf_seg), (cell_h, cell_s),
            (diag_h, diag), (mob_h, mob), (trans_h, trans), (rhs_h, rhs),
            (parent_h, parent), (seg_trans_h, seg_trans), (seg_rhs_h, seg_rhs),
        ])
    ]
    for load in loads:
        load.start()

    at_x = [my_x] + [lax.rem(my_x + a, nx) for a in range(1, nx)]
    at_y = [my_y] + [lax.rem(my_y + b, ny) for b in range(1, ny)]
    partners = [(at_x[a], at_y[b]) for b in range(ny) for a in range(nx) if a + b]

    xrecv[...] = jnp.zeros_like(xrecv)
    yrecv[...] = jnp.zeros_like(yrecv)
    for target in partners:
        pl.semaphore_signal(barrier, inc=1, device_id=target, device_id_type=MESH)

    has_x = [my_x > 0, my_x < nx - 1]
    has_y = [my_y > 0, my_y < ny - 1]

    def halos(slot):
        below_x, above_x = lax.max(my_x - 1, 0), lax.min(my_x + 1, nx - 1)
        below_y, above_y = lax.max(my_y - 1, 0), lax.min(my_y + 1, ny - 1)

        def copy(src, dst, way, device):
            return pltpu.make_async_remote_copy(
                src_ref=src, dst_ref=dst, send_sem=halo_send.at[slot, way],
                recv_sem=halo_recv.at[slot, way], device_id=device, device_id_type=MESH,
            )

        return [
            (has_x[1], has_x[0], copy(
                tx.at[:, :, SUB - 1:SUB, :], xrecv.at[slot, :, :, 0:1, :], 0, (above_x, my_y))),
            (has_x[0], has_x[1], copy(
                tx.at[:, :, 0:1, :], xrecv.at[slot, :, :, SUB - 1:SUB, :], 1, (below_x, my_y))),
            (has_y[1], has_y[0], copy(ypack.at[slot], yrecv.at[slot, 0], 2, (my_x, above_y))),
            (has_y[0], has_y[1], copy(ypack.at[slot], yrecv.at[slot, 1], 3, (my_x, below_y))),
        ]

    def send_halos(slot):
        for to, _, copy in halos(slot):
            pl.when(to)(copy.start)

    def wait_halos(slot):
        for to, come, copy in halos(slot):
            pl.when(come)(copy.wait_recv)
            pl.when(to)(copy.wait_send)

    def send_rows(slot):
        for target in partners:
            pos = target[0] * ny + target[1]
            pltpu.make_async_remote_copy(
                src_ref=send.at[slot, pl.ds(pos, 1), :], dst_ref=recv.at[slot, pl.ds(me, 1), :],
                send_sem=msg_send.at[slot], recv_sem=msg_recv.at[slot],
                device_id=target, device_id_type=MESH,
            ).start()

    def wait_rows(slot):
        some = pl.ds(0, n - 1)
        copy = pltpu.make_async_remote_copy(
            src_ref=send.at[slot, some, :], dst_ref=recv.at[slot, some, :],
            send_sem=msg_send.at[slot], recv_sem=msg_recv.at[slot],
            device_id=(my_x, my_y), device_id_type=MESH,
        )
        copy.wait_recv()
        copy.wait_send()

    row_n = lax.broadcasted_iota(jnp.int32, (n, LANE), 0)
    lane_n = lax.broadcasted_iota(jnp.int32, (n, LANE), 1)

    def arrived(slot):
        return jnp.where(row_n == me, send[slot], recv[slot])

    turn_i[...] = jnp.zeros_like(turn_i)
    turn_f[...] = jnp.zeros_like(turn_f)
    for load in loads[:4]:
        load.wait()
    turn_i[0:SLOTS, 0:n] = cell_v[0]
    turn_i[SLOTS:2 * SLOTS, 0:n] = perf_seg[0]
    turn_f[0:SLOTS, 0:n] = perf_pi[0]
    places = turn_i[...].T[0:n, :]
    weights = turn_f[...].T[0:n, :]
    send[0] = weights
    pl.semaphore_wait(barrier, n - 1)
    send_rows(0)

    lanes_at = lax.rem(places, LANE)
    idx[...] = lanes_at
    spread = jnp.zeros((n, LANE), F32)
    slot_of = jnp.zeros((n, LANE), jnp.int32)
    for k in range(SLOTS):
        here = lane_n == lanes_at[:, k:k + 1]
        spread = spread + jnp.where(here, weights[:, k:k + 1], 0.0)
        slot_of = jnp.where(here, SLOTS + k, slot_of)
    pi_row[...] = spread
    k_of[...] = slot_of
    row_id = lax.div(cell_v[0][0:1, :], LANE)
    row_id = jnp.concatenate([row_id] * 3, axis=1)
    grid_rows = lax.broadcasted_iota(jnp.int32, (layers * SUB, 3 * n), 0)
    onehot[...] = jnp.where(grid_rows == row_id, 1.0, 0.0).astype(jnp.bfloat16)
    same[...] = jnp.where(lax.div(places[:, 0:1], LANE) == row_id, 1.0, 0.0).astype(jnp.bfloat16)

    def split(field):
        high = field.astype(jnp.bfloat16)
        rest = field - high.astype(F32)
        mid = rest.astype(jnp.bfloat16)
        low = (rest - mid.astype(F32)).astype(jnp.bfloat16)
        return jnp.concatenate([high, mid, low], axis=0)

    def scatter():
        total = jnp.dot(onehot[...], flow[...], preferred_element_type=F32)
        into[...] = total.reshape(layers, SUB, LANE)

    flow[...] = split(spread)
    scatter()

    zc = 4 if layers % 4 == 0 else 1
    chunks = [slice(z, z + zc) for z in range(0, layers, zc)]
    lane = lax.broadcasted_iota(jnp.int32, (SUB, LANE), 1)
    row = lax.broadcasted_iota(jnp.int32, (SUB, LANE), 0)
    edge = (lane == 0) | (lane == LANE - 1)

    tz[:, 0] = jnp.zeros((3, SUB, LANE), F32)
    tz[:, layers + 1] = jnp.zeros((3, SUB, LANE), F32)

    def flat(zs):
        return slice(zs.start * SUB, zs.stop * SUB)

    def publish(zs, vec, packed):
        mv = apply3([mm[i, zs] for i in range(9)], vec)
        for c in range(3):
            v[c, flat(zs), :] = vec[c].reshape(zc * SUB, LANE)
            tx[c, zs] = tt[0, zs] * mv[c]
            along = tt[1, zs] * mv[c]
            ty[c, zs] = along
            tz[c, zs.start + 1:zs.stop + 1] = tt[2, zs] * mv[c]
            for z in range(zs.start, zs.stop):
                shift = (2 * (c * layers + z)) % LANE
                moved = along[z - zs.start]
                if shift:
                    moved = pltpu.roll(moved, shift, 1)
                mine = (lane == (shift - 1) % LANE) | (lane == shift)
                packed = jnp.where(mine, moved, packed)
        return packed

    for load in loads[4:]:
        load.wait()
    for zs in chunks:
        dense = [diag[i, zs].astype(F32) for i in range(9)]
        mobile = [mob[i, zs].astype(F32) for i in range(9)]
        inv = inverse3(dense)
        perf = into[zs]
        for i in range(9):
            dinv[i, zs] = inv[i]
            mm[i, zs] = mobile[i]
            dd[i, zs] = dense[i] + mobile[i] * perf if i % 3 == 0 else dense[i]
        for i in range(3):
            tt[i, zs] = trans[i, zs].astype(F32)
        ty_edge[zs] = jnp.where(edge, tt[1, zs], 0.0)
        gain = apply3(inv, [mobile[0], mobile[3], mobile[6]])
        vec = apply3(inv, [rhs[c, zs] for c in range(3)])
        for c in range(3):
            kk[c, flat(zs), :] = gain[c].reshape(zc * SUB, LANE)
            v[c, flat(zs), :] = vec[c].reshape(zc * SUB, LANE)
    flow[...] = jnp.zeros_like(flow)

    def pick_rows(source, target):
        for o in range(n):
            at = lax.div(cell_s[0, 0, o], LANE)
            target[o:o + 1, :] = source[0, pl.ds(at, 1), :]

    pick_rows(kk, k_rows)
    pick_rows(v, rows)

    seg[...] = jnp.zeros_like(seg)
    seg[0, 0:seg_rows, :] = jnp.where(parent[...] >= 0, seg_trans[...], 0.0)
    seg[2, 0:seg_rows, :] = seg_trans[...]
    seg[3, 0:seg_rows, :] = seg_rhs[...]

    def before(x):
        moved = pltpu.roll(x, 1, 1)
        return jnp.where(lane == 0, pltpu.roll(moved, 1, 0), moved)

    def after(x):
        moved = pltpu.roll(x, LANE - 1, 1)
        return jnp.where(lane == LANE - 1, pltpu.roll(moved, SUB - 1, 0), moved)

    def tile(parts):
        total = jnp.zeros((SUB, LANE), F32)
        for r in range(seg_rows):
            total = jnp.where(row == r, jnp.sum(parts[r], axis=0, keepdims=True), total)
        return total

    seg[1] = after(seg[0])
    wait_rows(0)
    came = arrived(0)
    parts = [jnp.zeros((n, LANE), F32) for _ in range(seg_rows)]
    for k in range(SLOTS):
        goes = places[:, SLOTS + k:SLOTS + k + 1]
        for r in range(seg_rows):
            term = jnp.where(lane_n + r * LANE == goes, came[:, k:k + 1], 0.0)
            feed[k, r] = term
            parts[r] = parts[r] + term
    turn_i[0:n, :] = lax.div(places, LANE)
    seg[2] = jnp.where(row < seg_rows, seg[2] + seg[1] + tile(parts), 1.0)
    seg[4] = seg[3] / seg[2]
    sums[...] = jnp.zeros_like(sums)

    def fill(slot):
        where_to = idx[...]
        which = turn_i[0:n, :]
        state = seg[4]
        there = rows[...] + k_rows[...] * jnp.dot(
            same[...], flow[...], preferred_element_type=F32)
        row_vals = jnp.take_along_axis(there, where_to, axis=1, mode="promise_in_bounds")
        seg_vals = jnp.zeros((n, LANE), F32)
        for r in range(seg_rows):
            whole = jnp.broadcast_to(state[r:r + 1, :], (n, LANE))
            got = jnp.take_along_axis(whole, where_to, axis=1, mode="promise_in_bounds")
            seg_vals = jnp.where(which == r, got, seg_vals)
        total = jnp.broadcast_to(sums[0:1, :], (n, LANE))
        send[slot] = jnp.where(
            lane_n < SLOTS, row_vals, jnp.where(lane_n < 2 * SLOTS, seg_vals, total))

    fill(1)

    def advance(slot):
        scatter()
        packed = jnp.zeros((SUB, LANE), F32)
        for zs in chunks:
            vec = [
                v[c, flat(zs), :].reshape(zc, SUB, LANE)
                + kk[c, flat(zs), :].reshape(zc, SUB, LANE) * into[zs]
                for c in range(3)
            ]
            packed = publish(zs, vec, packed)
        ypack[slot] = packed

    def inside():
        for zs in chunks:
            vec = [v[c, flat(zs), :].reshape(zc, SUB, LANE) for c in range(3)]
            pulled = apply3([dd[i, zs] for i in range(9)], vec)
            for c in range(3):
                x, y = tx[c, zs], ty[c, zs]
                near_x = (
                    jnp.where(row == 0, 0.0, pltpu.roll(x, 1, 1))
                    + jnp.where(row == SUB - 1, 0.0, pltpu.roll(x, SUB - 1, 1)))
                near_y = (
                    jnp.where(lane == 0, 0.0, pltpu.roll(y, 1, 2))
                    + jnp.where(lane == LANE - 1, 0.0, pltpu.roll(y, LANE - 1, 2)))
                near_z = tz[c, zs] + tz[c, zs.start + 2:zs.stop + 2]
                part[c, zs] = (
                    rhs[c, zs] - pulled[c]
                    + (tt[0, zs] * near_x + tt[1, zs] * near_y + tt[2, zs] * near_z))

    def segments(came):
        parts = [jnp.zeros((n, LANE), F32) for _ in range(seg_rows)]
        for k in range(SLOTS):
            value = jnp.broadcast_to(came[:, k:k + 1], (n, LANE))
            for r in range(seg_rows):
                parts[r] = parts[r] + value * feed[k, r]
        g = seg[4]
        return (
            seg[3] - seg[2] * g + seg[0] * before(g) + seg[1] * after(g) + tile(parts))

    def receive(slot):
        wait_rows(slot)
        came = arrived(slot)
        pressure = jnp.take_along_axis(came, k_of[...], axis=1, mode="promise_in_bounds")
        flow[...] = split(pi_row[...] * pressure)
        seg[5] = segments(came)
        return came

    def borders(slot, last):
        wait_halos(slot)
        border = jnp.where(
            lax.rem(lane, 2) == 0,
            pltpu.roll(yrecv[slot, 0], 1, 1), pltpu.roll(yrecv[slot, 1], LANE - 1, 1))
        for zs in chunks:
            vec = []
            for c in range(3):
                total = part[c, zs] + tt[0, zs] * xrecv[slot, c, zs]
                sides = []
                for z in range(zs.start, zs.stop):
                    shift = (2 * (c * layers + z)) % LANE
                    sides.append(pltpu.roll(border, LANE - shift, 1) if shift else border)
                total = total + ty_edge[zs] * jnp.stack(sides)
                res[c, zs] = total
                vec.append(total)
            if not last:
                step = apply3([dinv[i, zs] for i in range(9)], vec)
                for c in range(3):
                    v[c, flat(zs), :] = v[c, flat(zs), :] + step[c].reshape(zc * SUB, LANE)

    def put_sums(numer, denom):
        first = jnp.sum(jnp.sum(numer, axis=0, keepdims=True), axis=1, keepdims=True)
        second = jnp.sum(jnp.sum(denom, axis=0, keepdims=True), axis=1, keepdims=True)
        sums[...] = jnp.where(
            lane == 2 * SLOTS, first, jnp.where(lane == 2 * SLOTS + 1, second, 0.0))

    def ratio(came):
        total = jnp.sum(came, axis=0, keepdims=True)
        return total[:, 2 * SLOTS:2 * SLOTS + 1] / total[:, 2 * SLOTS + 1:2 * SLOTS + 2]

    def keep_state():
        for c in range(3):
            for zs in chunks:
                v4[c, zs] = v[c, flat(zs), :].reshape(zc, SUB, LANE)
        seg[6] = seg[4]

    def keep_residual():
        numer = seg[3] * (seg[3] - seg[5])
        denom = (seg[3] - seg[5]) * (seg[3] - seg[5])
        seg[7] = seg[5]
        for c in range(3):
            for zs in chunks:
                last, start = res[c, zs] + mm[3 * c, zs] * into[zs], rhs[c, zs]
                a4[c, zs] = last
                diff = start - last
                numer = numer + jnp.sum(start * diff, axis=0)
                denom = denom + jnp.sum(diff * diff, axis=0)
        put_sums(numer, denom)

    def exchange(k, slot, last):
        send_rows(slot)
        advance(slot)
        send_halos(slot)
        pl.when(k == SWEEPS)(keep_state)
        pl.when(k == SWEEPS + 1)(keep_residual)
        inside()
        borders(slot, last)

    def sweep(k, carry):
        slot = lax.rem(k, 2)
        exchange(k, slot, False)
        pick_rows(v, rows)
        came = receive(slot)

        @pl.when(k == SWEEPS + 2)
        def _():
            sums[1:2, :] = jnp.broadcast_to(ratio(came), (1, LANE))

        seg[4] = seg[4] + seg[5] / seg[2]
        fill(1 - slot)
        return carry

    last = 2 * SWEEPS
    lax.fori_loop(1, last, sweep, 0)
    slot = last % 2
    omega = sums[1:2, :]
    exchange(last, slot, True)
    receive(slot)
    scatter()

    def mix(old, new):
        return old + omega * (new - old)

    start, middle, end = seg[3], seg[7], seg[5]
    first = mix(start, middle)
    diff = first - mix(middle, end)
    numer, denom = first * diff, diff * diff
    for zs in chunks:
        for c in range(3):
            middle = a4[c, zs]
            first = mix(rhs[c, zs], middle)
            diff = first - mix(middle, res[c, zs] + mm[3 * c, zs] * into[zs])
            numer = numer + jnp.sum(first * diff, axis=0)
            denom = denom + jnp.sum(diff * diff, axis=0)
    put_sums(numer, denom)
    send[1] = jnp.broadcast_to(sums[0:1, :], (n, LANE))
    send_rows(1)
    wait_rows(1)
    second = jnp.broadcast_to(ratio(arrived(1)), (1, LANE))

    def combine(middle, end):
        base = omega * middle
        return base + second * (mix(middle, end) - base)

    for c in range(3):
        for zs in chunks:
            out_u[c, zs] = combine(v4[c, zs], v[c, flat(zs), :].reshape(zc, SUB, LANE))
    out_w[...] = combine(seg[6], seg[4])[0:seg_rows, :]


def on_device(
    rhs, diag_block, mobility, trans, perf_cell, perf_pi, perf_seg, seg_parent, seg_trans, seg_rhs
):
    nx, ny = lax.axis_size("gx"), lax.axis_size("gy")
    n = nx * ny
    layers = rhs.shape[1]
    seg_rows = seg_rhs.shape[0] // LANE
    tiles = (seg_rows, LANE)
    cells = (layers, SUB, LANE)
    vmem = pl.BlockSpec(memory_space=pltpu.VMEM)
    far = pl.BlockSpec(memory_space=pltpu.HBM)

    def scratch(*shape, kind=F32):
        return pltpu.VMEM(shape, kind)

    slots = perf_cell.shape
    half, whole = jnp.bfloat16, jnp.int32
    u, w = pl.pallas_call(
        functools.partial(kernel, nx, ny, layers, seg_rows),
        out_shape=[
            jax.ShapeDtypeStruct(rhs.shape, F32), jax.ShapeDtypeStruct(tiles, F32)],
        in_specs=[far] * 10,
        out_specs=[vmem] * 2,
        scratch_shapes=[
            scratch(3, *cells), scratch(9, *cells, kind=half), scratch(9, *cells, kind=half),
            scratch(3, *cells, kind=half), pltpu.SMEM(slots, whole),
            scratch(*slots, kind=whole), scratch(*slots), scratch(*slots, kind=whole),
            scratch(*tiles, kind=whole), scratch(*tiles), scratch(*tiles),
            scratch(3, layers * SUB, LANE), scratch(3, *cells), scratch(3, *cells),
            scratch(3, layers + 2, SUB, LANE), scratch(3, *cells), scratch(3, *cells),
            scratch(3, *cells), scratch(3, *cells), scratch(9, *cells), scratch(9, *cells),
            scratch(9, *cells), scratch(3, layers * SUB, LANE), scratch(3, *cells),
            scratch(*cells), scratch(*cells),
            scratch(layers * SUB, 3 * n, kind=half), scratch(n, 3 * n, kind=half),
            scratch(SLOTS, seg_rows, n, LANE), scratch(n, LANE),
            scratch(n, LANE, kind=whole), scratch(n, LANE, kind=whole),
            scratch(n, LANE), scratch(n, LANE), scratch(3 * n, LANE, kind=half),
            scratch(2, n, LANE), scratch(2, n, LANE),
            scratch(2, SUB, LANE), scratch(2, 2, SUB, LANE), scratch(2, 3, *cells),
            scratch(LANE, LANE, kind=whole), scratch(LANE, LANE),
            scratch(8, SUB, LANE), scratch(SUB, LANE),
            pltpu.SemaphoreType.DMA((2, 4)), pltpu.SemaphoreType.DMA((2, 4)),
            pltpu.SemaphoreType.DMA((2,)), pltpu.SemaphoreType.DMA((2,)),
            pltpu.SemaphoreType.DMA((11,)),
        ],
        compiler_params=pltpu.CompilerParams(
            collective_id=0, has_side_effects=True, vmem_limit_bytes=40 * 1024 * 1024),
        name="sweeps",
    )(
        rhs, diag_block, mobility, trans, perf_cell, perf_pi, perf_seg,
        seg_parent.reshape(tiles), seg_trans.reshape(tiles), seg_rhs.reshape(tiles),
    )
    return u, w.reshape(-1)


def solution(mesh):
    return jax.shard_map(
        on_device,
        mesh=mesh,
        in_specs=(
            P(None, None, "gx", "gy"),
            P(None, None, "gx", "gy"),
            P(None, None, "gx", "gy"),
            P(None, None, "gx", "gy"),
            P(("gx", "gy"), None, None),
            P(("gx", "gy"), None, None),
            P(("gx", "gy"), None, None),
            P(("gx", "gy")),
            P(("gx", "gy")),
            P(("gx", "gy")),
        ),
        out_specs=(P(None, None, "gx", "gy"), P(("gx", "gy"))),
        check_vma=False,
    )
```

```python
import functools

import jax
import jax.numpy as jnp
from jax import lax
from jax.experimental import pallas as pl
from jax.experimental.pallas import tpu as pltpu
from jax.sharding import PartitionSpec as P

SWEEPS = 4
SUB, LANE = 8, 128
SLOTS = 8
MESH = pl.DeviceIdType.MESH
F32 = jnp.float32


def apply3(mat, vec):
    return [mat[3 * r] * vec[0] + mat[3 * r + 1] * vec[1] + mat[3 * r + 2] * vec[2] for r in range(3)]


def inverse3(m):
    a, b, c, d, e, f, g, h, i = m
    first = e * i - f * h
    second = f * g - d * i
    third = d * h - e * g
    inv = 1.0 / (a * first + b * second + c * third)
    entries = [
        first, c * h - b * i, b * f - c * e,
        second, a * i - c * g, c * d - a * f,
        third, b * g - a * h, a * e - b * d,
    ]
    return [entry * inv for entry in entries]


def kernel(
    nx, ny, layers, seg_rows,
    rhs_h, diag_h, mob_h, trans_h, cell_h, pi_h, seg_h, parent_h, seg_trans_h, seg_rhs_h,
    out_u, out_w,
    rhs, diag, mob, trans, cell_s, cell_v, perf_pi, perf_seg, parent, seg_trans, seg_rhs,
    v, tx, ty, tz, part, res, v4, a4, dinv, dd, mm, kk, tt, ty_edge, into,
    onehot, same, feed, pi_row, k_of, idx, rows, k_rows, flow, send, hop, recv, ypack, yrecv, xrecv,
    turn_i, turn_f, seg, sums,
    halo_send, halo_recv, msg_send, msg_recv, load_sem,
):
    n = nx * ny
    my_x, my_y = lax.axis_index("gx"), lax.axis_index("gy")
    me = my_x * ny + my_y
    barrier = pltpu.get_barrier_semaphore()

    loads = [
        pltpu.make_async_copy(src, dst, load_sem.at[i])
        for i, (src, dst) in enumerate([
            (cell_h, cell_v), (pi_h, perf_pi), (seg_h, perf_seg), (cell_h, cell_s),
            (diag_h, diag), (mob_h, mob), (trans_h, trans), (rhs_h, rhs),
            (parent_h, parent), (seg_trans_h, seg_trans), (seg_rhs_h, seg_rhs),
        ])
    ]
    for load in loads:
        load.start()

    at_x = [my_x] + [lax.rem(my_x + a, nx) for a in range(1, nx)]
    at_y = [my_y] + [lax.rem(my_y + b, ny) for b in range(1, ny)]
    partners = [(x, my_y) for x in at_x[1:]] + [(my_x, y) for y in at_y[1:]]

    xrecv[...] = jnp.zeros_like(xrecv)
    yrecv[...] = jnp.zeros_like(yrecv)
    for target in partners:
        pl.semaphore_signal(barrier, inc=1, device_id=target, device_id_type=MESH)

    has_x = [my_x > 0, my_x < nx - 1]
    has_y = [my_y > 0, my_y < ny - 1]

    def halos(slot):
        below_x, above_x = lax.max(my_x - 1, 0), lax.min(my_x + 1, nx - 1)
        below_y, above_y = lax.max(my_y - 1, 0), lax.min(my_y + 1, ny - 1)

        def copy(src, dst, way, device):
            return pltpu.make_async_remote_copy(
                src_ref=src, dst_ref=dst, send_sem=halo_send.at[slot, way],
                recv_sem=halo_recv.at[slot, way], device_id=device, device_id_type=MESH,
            )

        return [
            (has_x[1], has_x[0], copy(
                tx.at[:, :, SUB - 1:SUB, :], xrecv.at[slot, :, :, 0:1, :], 0, (above_x, my_y))),
            (has_x[0], has_x[1], copy(
                tx.at[:, :, 0:1, :], xrecv.at[slot, :, :, SUB - 1:SUB, :], 1, (below_x, my_y))),
            (has_y[1], has_y[0], copy(ypack.at[slot], yrecv.at[slot, 0], 2, (my_x, above_y))),
            (has_y[0], has_y[1], copy(ypack.at[slot], yrecv.at[slot, 1], 3, (my_x, below_y))),
        ]

    def send_halos(slot):
        for to, _, copy in halos(slot):
            pl.when(to)(copy.start)

    def wait_halos(slot):
        for to, come, copy in halos(slot):
            pl.when(come)(copy.wait_recv)
            pl.when(to)(copy.wait_send)

    def step_copy(slot, step, src, dst, device):
        return pltpu.make_async_remote_copy(
            src_ref=src, dst_ref=dst, send_sem=msg_send.at[slot, step],
            recv_sem=msg_recv.at[slot, step], device_id=device, device_id_type=MESH,
        )

    def put_rows(slot, values):
        send[slot] = values.reshape(nx, ny, LANE)
        hop[slot, my_x] = send[slot, my_x]

    def send_rows(slot):
        for x in at_x[1:]:
            step_copy(slot, 0, send.at[slot, x], hop.at[slot, my_x], (x, my_y)).start()

    def pass_rows(slot):
        some = pl.ds(0, nx - 1)
        copy = step_copy(slot, 0, send.at[slot, some], hop.at[slot, some], (my_x, my_y))
        copy.wait_recv()
        copy.wait_send()
        for y in at_y[1:]:
            step_copy(
                slot, 1, hop.at[slot, :, pl.ds(y, 1), :], recv.at[slot, :, pl.ds(my_y, 1), :],
                (my_x, y)).start()

    def wait_rows(slot):
        some = pl.ds(0, ny - 1)
        copy = step_copy(
            slot, 1, hop.at[slot, :, some, :], recv.at[slot, :, some, :], (my_x, my_y))
        copy.wait_recv()
        copy.wait_send()

    lane_n = lax.broadcasted_iota(jnp.int32, (n, LANE), 1)

    def arrived(slot):
        from_y = lax.broadcasted_iota(jnp.int32, (nx, ny, LANE), 1)
        return jnp.where(from_y == my_y, hop[slot], recv[slot]).reshape(n, LANE)

    turn_i[...] = jnp.zeros_like(turn_i)
    turn_f[...] = jnp.zeros_like(turn_f)
    for load in loads[:4]:
        load.wait()
    turn_i[0:SLOTS, 0:n] = cell_v[0]
    turn_i[SLOTS:2 * SLOTS, 0:n] = perf_seg[0]
    turn_f[0:SLOTS, 0:n] = perf_pi[0]
    places = turn_i[...].T[0:n, :]
    weights = turn_f[...].T[0:n, :]
    put_rows(0, weights)
    pl.semaphore_wait(barrier, nx + ny - 2)
    send_rows(0)

    lanes_at = lax.rem(places, LANE)
    idx[...] = lanes_at
    spread = jnp.zeros((n, LANE), F32)
    slot_of = jnp.zeros((n, LANE), jnp.int32)
    for k in range(SLOTS):
        here = lane_n == lanes_at[:, k:k + 1]
        spread = spread + jnp.where(here, weights[:, k:k + 1], 0.0)
        slot_of = jnp.where(here, SLOTS + k, slot_of)
    pi_row[...] = spread
    k_of[...] = slot_of
    row_id = lax.div(cell_v[0][0:1, :], LANE)
    row_id = jnp.concatenate([row_id] * 3, axis=1)
    grid_rows = lax.broadcasted_iota(jnp.int32, (layers * SUB, 3 * n), 0)
    onehot[...] = jnp.where(grid_rows == row_id, 1.0, 0.0).astype(jnp.bfloat16)
    same[...] = jnp.where(lax.div(places[:, 0:1], LANE) == row_id, 1.0, 0.0).astype(jnp.bfloat16)

    def split(field):
        high = field.astype(jnp.bfloat16)
        rest = field - high.astype(F32)
        mid = rest.astype(jnp.bfloat16)
        low = (rest - mid.astype(F32)).astype(jnp.bfloat16)
        return jnp.concatenate([high, mid, low], axis=0)

    def scatter():
        total = jnp.dot(onehot[...], flow[...], preferred_element_type=F32)
        into[...] = total.reshape(layers, SUB, LANE)

    flow[...] = split(spread)
    scatter()
    pass_rows(0)

    zc = 4 if layers % 4 == 0 else 1
    chunks = [slice(z, z + zc) for z in range(0, layers, zc)]
    lane = lax.broadcasted_iota(jnp.int32, (SUB, LANE), 1)
    row = lax.broadcasted_iota(jnp.int32, (SUB, LANE), 0)
    edge = (lane == 0) | (lane == LANE - 1)

    tz[:, 0] = jnp.zeros((3, SUB, LANE), F32)
    tz[:, layers + 1] = jnp.zeros((3, SUB, LANE), F32)

    def flat(zs):
        return slice(zs.start * SUB, zs.stop * SUB)

    def publish(zs, vec, packed):
        mv = apply3([mm[i, zs] for i in range(9)], vec)
        for c in range(3):
            v[c, flat(zs), :] = vec[c].reshape(zc * SUB, LANE)
            tx[c, zs] = tt[0, zs] * mv[c]
            along = tt[1, zs] * mv[c]
            ty[c, zs] = along
            tz[c, zs.start + 1:zs.stop + 1] = tt[2, zs] * mv[c]
            for z in range(zs.start, zs.stop):
                shift = (2 * (c * layers + z)) % LANE
                moved = along[z - zs.start]
                if shift:
                    moved = pltpu.roll(moved, shift, 1)
                mine = (lane == (shift - 1) % LANE) | (lane == shift)
                packed = jnp.where(mine, moved, packed)
        return packed

    for load in loads[4:]:
        load.wait()
    for zs in chunks:
        dense = [diag[i, zs].astype(F32) for i in range(9)]
        mobile = [mob[i, zs].astype(F32) for i in range(9)]
        inv = inverse3(dense)
        perf = into[zs]
        for i in range(9):
            dinv[i, zs] = inv[i]
            mm[i, zs] = mobile[i]
            dd[i, zs] = dense[i] + mobile[i] * perf if i % 3 == 0 else dense[i]
        for i in range(3):
            tt[i, zs] = trans[i, zs].astype(F32)
        ty_edge[zs] = jnp.where(edge, tt[1, zs], 0.0)
        gain = apply3(inv, [mobile[0], mobile[3], mobile[6]])
        vec = apply3(inv, [rhs[c, zs] for c in range(3)])
        for c in range(3):
            kk[c, flat(zs), :] = gain[c].reshape(zc * SUB, LANE)
            v[c, flat(zs), :] = vec[c].reshape(zc * SUB, LANE)
    flow[...] = jnp.zeros_like(flow)

    def pick_rows(source, target):
        for o in range(n):
            at = lax.div(cell_s[0, 0, o], LANE)
            target[o:o + 1, :] = source[0, pl.ds(at, 1), :]

    pick_rows(kk, k_rows)
    pick_rows(v, rows)

    seg[...] = jnp.zeros_like(seg)
    seg[0, 0:seg_rows, :] = jnp.where(parent[...] >= 0, seg_trans[...], 0.0)
    seg[2, 0:seg_rows, :] = seg_trans[...]
    seg[3, 0:seg_rows, :] = seg_rhs[...]

    def before(x):
        moved = pltpu.roll(x, 1, 1)
        return jnp.where(lane == 0, pltpu.roll(moved, 1, 0), moved)

    def after(x):
        moved = pltpu.roll(x, LANE - 1, 1)
        return jnp.where(lane == LANE - 1, pltpu.roll(moved, SUB - 1, 0), moved)

    def tile(parts):
        total = jnp.zeros((SUB, LANE), F32)
        for r in range(seg_rows):
            total = jnp.where(row == r, jnp.sum(parts[r], axis=0, keepdims=True), total)
        return total

    seg[1] = after(seg[0])
    wait_rows(0)
    came = arrived(0)
    parts = [jnp.zeros((n, LANE), F32) for _ in range(seg_rows)]
    for k in range(SLOTS):
        goes = places[:, SLOTS + k:SLOTS + k + 1]
        for r in range(seg_rows):
            term = jnp.where(lane_n + r * LANE == goes, came[:, k:k + 1], 0.0)
            feed[k, r] = term
            parts[r] = parts[r] + term
    turn_i[0:n, :] = lax.div(places, LANE)
    seg[2] = jnp.where(row < seg_rows, seg[2] + seg[1] + tile(parts), 1.0)
    seg[4] = seg[3] / seg[2]
    sums[...] = jnp.zeros_like(sums)

    def fill(slot):
        where_to = idx[...]
        which = turn_i[0:n, :]
        state = seg[4]
        there = rows[...] + k_rows[...] * jnp.dot(
            same[...], flow[...], preferred_element_type=F32)
        row_vals = jnp.take_along_axis(there, where_to, axis=1, mode="promise_in_bounds")
        seg_vals = jnp.zeros((n, LANE), F32)
        for r in range(seg_rows):
            whole = jnp.broadcast_to(state[r:r + 1, :], (n, LANE))
            got = jnp.take_along_axis(whole, where_to, axis=1, mode="promise_in_bounds")
            seg_vals = jnp.where(which == r, got, seg_vals)
        total = jnp.broadcast_to(sums[0:1, :], (n, LANE))
        put_rows(slot, jnp.where(
            lane_n < SLOTS, row_vals, jnp.where(lane_n < 2 * SLOTS, seg_vals, total)))

    fill(1)

    def advance(slot):
        scatter()
        packed = jnp.zeros((SUB, LANE), F32)
        for zs in chunks:
            vec = [
                v[c, flat(zs), :].reshape(zc, SUB, LANE)
                + kk[c, flat(zs), :].reshape(zc, SUB, LANE) * into[zs]
                for c in range(3)
            ]
            packed = publish(zs, vec, packed)
        ypack[slot] = packed

    def inside(chunks):
        for zs in chunks:
            vec = [v[c, flat(zs), :].reshape(zc, SUB, LANE) for c in range(3)]
            pulled = apply3([dd[i, zs] for i in range(9)], vec)
            for c in range(3):
                x, y = tx[c, zs], ty[c, zs]
                near_x = (
                    jnp.where(row == 0, 0.0, pltpu.roll(x, 1, 1))
                    + jnp.where(row == SUB - 1, 0.0, pltpu.roll(x, SUB - 1, 1)))
                near_y = (
                    jnp.where(lane == 0, 0.0, pltpu.roll(y, 1, 2))
                    + jnp.where(lane == LANE - 1, 0.0, pltpu.roll(y, LANE - 1, 2)))
                near_z = tz[c, zs] + tz[c, zs.start + 2:zs.stop + 2]
                part[c, zs] = (
                    rhs[c, zs] - pulled[c]
                    + (tt[0, zs] * near_x + tt[1, zs] * near_y + tt[2, zs] * near_z))

    def segments(came):
        parts = [jnp.zeros((n, LANE), F32) for _ in range(seg_rows)]
        for k in range(SLOTS):
            value = jnp.broadcast_to(came[:, k:k + 1], (n, LANE))
            for r in range(seg_rows):
                parts[r] = parts[r] + value * feed[k, r]
        g = seg[4]
        return (
            seg[3] - seg[2] * g + seg[0] * before(g) + seg[1] * after(g) + tile(parts))

    def receive(slot):
        wait_rows(slot)
        came = arrived(slot)
        pressure = jnp.take_along_axis(came, k_of[...], axis=1, mode="promise_in_bounds")
        flow[...] = split(pi_row[...] * pressure)
        seg[5] = segments(came)
        return came

    def borders(slot, last):
        wait_halos(slot)
        border = jnp.where(
            lax.rem(lane, 2) == 0,
            pltpu.roll(yrecv[slot, 0], 1, 1), pltpu.roll(yrecv[slot, 1], LANE - 1, 1))
        for zs in chunks:
            vec = []
            for c in range(3):
                total = part[c, zs] + tt[0, zs] * xrecv[slot, c, zs]
                sides = []
                for z in range(zs.start, zs.stop):
                    shift = (2 * (c * layers + z)) % LANE
                    sides.append(pltpu.roll(border, LANE - shift, 1) if shift else border)
                total = total + ty_edge[zs] * jnp.stack(sides)
                res[c, zs] = total
                vec.append(total)
            if not last:
                step = apply3([dinv[i, zs] for i in range(9)], vec)
                for c in range(3):
                    v[c, flat(zs), :] = v[c, flat(zs), :] + step[c].reshape(zc * SUB, LANE)

    def put_sums(numer, denom):
        first = jnp.sum(jnp.sum(numer, axis=0, keepdims=True), axis=1, keepdims=True)
        second = jnp.sum(jnp.sum(denom, axis=0, keepdims=True), axis=1, keepdims=True)
        sums[...] = jnp.where(
            lane == 2 * SLOTS, first, jnp.where(lane == 2 * SLOTS + 1, second, 0.0))

    def ratio(came):
        total = jnp.sum(came, axis=0, keepdims=True)
        return total[:, 2 * SLOTS:2 * SLOTS + 1] / total[:, 2 * SLOTS + 1:2 * SLOTS + 2]

    def keep_state():
        for c in range(3):
            for zs in chunks:
                v4[c, zs] = v[c, flat(zs), :].reshape(zc, SUB, LANE)
        seg[6] = seg[4]

    def keep_residual():
        numer = seg[3] * (seg[3] - seg[5])
        denom = (seg[3] - seg[5]) * (seg[3] - seg[5])
        seg[7] = seg[5]
        for c in range(3):
            for zs in chunks:
                last, start = res[c, zs] + mm[3 * c, zs] * into[zs], rhs[c, zs]
                a4[c, zs] = last
                diff = start - last
                numer = numer + jnp.sum(start * diff, axis=0)
                denom = denom + jnp.sum(diff * diff, axis=0)
        put_sums(numer, denom)

    def exchange(k, slot, last):
        send_rows(slot)
        advance(slot)
        send_halos(slot)
        pl.when(k == SWEEPS)(keep_state)
        pl.when(k == SWEEPS + 1)(keep_residual)
        inside(chunks[:2])
        pass_rows(slot)
        inside(chunks[2:])
        borders(slot, last)

    def sweep(k, carry):
        slot = lax.rem(k, 2)
        exchange(k, slot, False)
        pick_rows(v, rows)
        came = receive(slot)

        @pl.when(k == SWEEPS + 2)
        def _():
            sums[1:2, :] = jnp.broadcast_to(ratio(came), (1, LANE))

        seg[4] = seg[4] + seg[5] / seg[2]
        fill(1 - slot)
        return carry

    last = 2 * SWEEPS
    lax.fori_loop(1, last, sweep, 0)
    slot = last % 2
    omega = sums[1:2, :]
    exchange(last, slot, True)
    receive(slot)
    scatter()

    def mix(old, new):
        return old + omega * (new - old)

    start, middle, end = seg[3], seg[7], seg[5]
    first = mix(start, middle)
    diff = first - mix(middle, end)
    numer, denom = first * diff, diff * diff
    for zs in chunks:
        for c in range(3):
            middle = a4[c, zs]
            first = mix(rhs[c, zs], middle)
            diff = first - mix(middle, res[c, zs] + mm[3 * c, zs] * into[zs])
            numer = numer + jnp.sum(first * diff, axis=0)
            denom = denom + jnp.sum(diff * diff, axis=0)
    put_sums(numer, denom)
    put_rows(1, jnp.broadcast_to(sums[0:1, :], (n, LANE)))
    send_rows(1)
    pass_rows(1)
    wait_rows(1)
    second = jnp.broadcast_to(ratio(arrived(1)), (1, LANE))

    def combine(middle, end):
        base = omega * middle
        return base + second * (mix(middle, end) - base)

    for c in range(3):
        for zs in chunks:
            out_u[c, zs] = combine(v4[c, zs], v[c, flat(zs), :].reshape(zc, SUB, LANE))
    out_w[...] = combine(seg[6], seg[4])[0:seg_rows, :]


def on_device(
    rhs, diag_block, mobility, trans, perf_cell, perf_pi, perf_seg, seg_parent, seg_trans, seg_rhs
):
    nx, ny = lax.axis_size("gx"), lax.axis_size("gy")
    n = nx * ny
    layers = rhs.shape[1]
    seg_rows = seg_rhs.shape[0] // LANE
    tiles = (seg_rows, LANE)
    cells = (layers, SUB, LANE)
    vmem = pl.BlockSpec(memory_space=pltpu.VMEM)
    far = pl.BlockSpec(memory_space=pltpu.HBM)

    def scratch(*shape, kind=F32):
        return pltpu.VMEM(shape, kind)

    slots = perf_cell.shape
    half, whole = jnp.bfloat16, jnp.int32
    u, w = pl.pallas_call(
        functools.partial(kernel, nx, ny, layers, seg_rows),
        out_shape=[
            jax.ShapeDtypeStruct(rhs.shape, F32), jax.ShapeDtypeStruct(tiles, F32)],
        in_specs=[far] * 10,
        out_specs=[vmem] * 2,
        scratch_shapes=[
            scratch(3, *cells), scratch(9, *cells, kind=half), scratch(9, *cells, kind=half),
            scratch(3, *cells, kind=half), pltpu.SMEM(slots, whole),
            scratch(*slots, kind=whole), scratch(*slots), scratch(*slots, kind=whole),
            scratch(*tiles, kind=whole), scratch(*tiles), scratch(*tiles),
            scratch(3, layers * SUB, LANE), scratch(3, *cells), scratch(3, *cells),
            scratch(3, layers + 2, SUB, LANE), scratch(3, *cells), scratch(3, *cells),
            scratch(3, *cells), scratch(3, *cells), scratch(9, *cells), scratch(9, *cells),
            scratch(9, *cells), scratch(3, layers * SUB, LANE), scratch(3, *cells),
            scratch(*cells), scratch(*cells),
            scratch(layers * SUB, 3 * n, kind=half), scratch(n, 3 * n, kind=half),
            scratch(SLOTS, seg_rows, n, LANE), scratch(n, LANE),
            scratch(n, LANE, kind=whole), scratch(n, LANE, kind=whole),
            scratch(n, LANE), scratch(n, LANE), scratch(3 * n, LANE, kind=half),
            scratch(2, nx, ny, LANE), scratch(2, nx, ny, LANE), scratch(2, nx, ny, LANE),
            scratch(2, SUB, LANE), scratch(2, 2, SUB, LANE), scratch(2, 3, *cells),
            scratch(LANE, LANE, kind=whole), scratch(LANE, LANE),
            scratch(8, SUB, LANE), scratch(SUB, LANE),
            pltpu.SemaphoreType.DMA((2, 4)), pltpu.SemaphoreType.DMA((2, 4)),
            pltpu.SemaphoreType.DMA((2, 2)), pltpu.SemaphoreType.DMA((2, 2)),
            pltpu.SemaphoreType.DMA((11,)),
        ],
        compiler_params=pltpu.CompilerParams(
            collective_id=0, has_side_effects=True, vmem_limit_bytes=62 * 1024 * 1024),
        name="sweeps",
    )(
        rhs, diag_block, mobility, trans, perf_cell, perf_pi, perf_seg,
        seg_parent.reshape(tiles), seg_trans.reshape(tiles), seg_rhs.reshape(tiles),
    )
    return u, w.reshape(-1)


def solution(mesh):
    return jax.shard_map(
        on_device,
        mesh=mesh,
        in_specs=(
            P(None, None, "gx", "gy"),
            P(None, None, "gx", "gy"),
            P(None, None, "gx", "gy"),
            P(None, None, "gx", "gy"),
            P(("gx", "gy"), None, None),
            P(("gx", "gy"), None, None),
            P(("gx", "gy"), None, None),
            P(("gx", "gy")),
            P(("gx", "gy")),
            P(("gx", "gy")),
        ),
        out_specs=(P(None, None, "gx", "gy"), P(("gx", "gy"))),
        check_vma=False,
    )
```

```python
import functools

import jax
import jax.numpy as jnp
from jax import lax
from jax.experimental import pallas as pl
from jax.experimental.pallas import tpu as pltpu
from jax.sharding import PartitionSpec as P

SWEEPS = 4
SUB, LANE = 8, 128
SLOTS = 8
MESH = pl.DeviceIdType.MESH
F32 = jnp.float32


def apply3(mat, vec):
    return [mat[3 * r] * vec[0] + mat[3 * r + 1] * vec[1] + mat[3 * r + 2] * vec[2] for r in range(3)]


def inverse3(m):
    a, b, c, d, e, f, g, h, i = m
    first = e * i - f * h
    second = f * g - d * i
    third = d * h - e * g
    inv = 1.0 / (a * first + b * second + c * third)
    entries = [
        first, c * h - b * i, b * f - c * e,
        second, a * i - c * g, c * d - a * f,
        third, b * g - a * h, a * e - b * d,
    ]
    return [entry * inv for entry in entries]


def kernel(
    nx, ny, layers, seg_rows,
    rhs_h, diag_h, mob_h, trans_h, cell_h, pi_h, seg_h, parent_h, seg_trans_h, seg_rhs_h,
    out_u, out_w,
    rhs, diag, mob, trans, cell_s, cell_v, perf_pi, perf_seg, parent, seg_trans, seg_rhs,
    v, tx, ty, tz, part, res, v4, a4, dinv, dd, mm, kk, tt, ty_edge, into,
    onehot, same, feed, pi_row, k_of, idx, rows, k_rows, flow, send, recv, ypack, yrecv, xrecv,
    turn_i, turn_f, seg, sums,
    halo_send, halo_recv, msg_send, msg_recv, load_sem,
):
    n = nx * ny
    my_x, my_y = lax.axis_index("gx"), lax.axis_index("gy")
    me = my_x * ny + my_y
    barrier = pltpu.get_barrier_semaphore()

    loads = [
        pltpu.make_async_copy(src, dst, load_sem.at[i])
        for i, (src, dst) in enumerate([
            (cell_h, cell_v), (pi_h, perf_pi), (seg_h, perf_seg), (cell_h, cell_s),
            (diag_h, diag), (mob_h, mob), (trans_h, trans), (rhs_h, rhs),
            (parent_h, parent), (seg_trans_h, seg_trans), (seg_rhs_h, seg_rhs),
        ])
    ]
    for load in loads:
        load.start()

    at_x = [my_x] + [lax.rem(my_x + a, nx) for a in range(1, nx)]
    at_y = [my_y] + [lax.rem(my_y + b, ny) for b in range(1, ny)]
    far_first = sorted(range(ny), key=lambda b: -min(b, ny - b))
    partners = [(at_x[a], at_y[b]) for b in far_first for a in reversed(range(nx)) if a + b]

    xrecv[...] = jnp.zeros_like(xrecv)
    yrecv[...] = jnp.zeros_like(yrecv)
    for target in partners:
        pl.semaphore_signal(barrier, inc=1, device_id=target, device_id_type=MESH)

    has_x = [my_x > 0, my_x < nx - 1]
    has_y = [my_y > 0, my_y < ny - 1]

    def halos(slot):
        below_x, above_x = lax.max(my_x - 1, 0), lax.min(my_x + 1, nx - 1)
        below_y, above_y = lax.max(my_y - 1, 0), lax.min(my_y + 1, ny - 1)

        def copy(src, dst, way, device):
            return pltpu.make_async_remote_copy(
                src_ref=src, dst_ref=dst, send_sem=halo_send.at[slot, way],
                recv_sem=halo_recv.at[slot, way], device_id=device, device_id_type=MESH,
            )

        return [
            (has_x[1], has_x[0], copy(
                tx.at[:, :, SUB - 1:SUB, :], xrecv.at[slot, :, :, 0:1, :], 0, (above_x, my_y))),
            (has_x[0], has_x[1], copy(
                tx.at[:, :, 0:1, :], xrecv.at[slot, :, :, SUB - 1:SUB, :], 1, (below_x, my_y))),
            (has_y[1], has_y[0], copy(ypack.at[slot], yrecv.at[slot, 0], 2, (my_x, above_y))),
            (has_y[0], has_y[1], copy(ypack.at[slot], yrecv.at[slot, 1], 3, (my_x, below_y))),
        ]

    def send_halos(slot):
        for to, _, copy in halos(slot):
            pl.when(to)(copy.start)

    def wait_halos(slot):
        for to, come, copy in halos(slot):
            pl.when(come)(copy.wait_recv)
            pl.when(to)(copy.wait_send)

    def send_rows(slot):
        for target in partners:
            pos = target[0] * ny + target[1]
            pltpu.make_async_remote_copy(
                src_ref=send.at[slot, pl.ds(pos, 1), :], dst_ref=recv.at[slot, pl.ds(me, 1), :],
                send_sem=msg_send.at[slot], recv_sem=msg_recv.at[slot],
                device_id=target, device_id_type=MESH,
            ).start()

    def wait_rows(slot):
        some = pl.ds(0, n - 1)
        copy = pltpu.make_async_remote_copy(
            src_ref=send.at[slot, some, :], dst_ref=recv.at[slot, some, :],
            send_sem=msg_send.at[slot], recv_sem=msg_recv.at[slot],
            device_id=(my_x, my_y), device_id_type=MESH,
        )
        copy.wait_recv()
        copy.wait_send()

    row_n = lax.broadcasted_iota(jnp.int32, (n, LANE), 0)
    lane_n = lax.broadcasted_iota(jnp.int32, (n, LANE), 1)

    def arrived(slot):
        return jnp.where(row_n == me, send[slot], recv[slot])

    turn_i[...] = jnp.zeros_like(turn_i)
    turn_f[...] = jnp.zeros_like(turn_f)
    for load in loads[:4]:
        load.wait()
    turn_i[0:SLOTS, 0:n] = cell_v[0]
    turn_i[SLOTS:2 * SLOTS, 0:n] = perf_seg[0]
    turn_f[0:SLOTS, 0:n] = perf_pi[0]
    places = turn_i[...].T[0:n, :]
    weights = turn_f[...].T[0:n, :]
    send[0] = weights
    pl.semaphore_wait(barrier, n - 1)
    send_rows(0)

    lanes_at = lax.rem(places, LANE)
    idx[...] = lanes_at
    spread = jnp.zeros((n, LANE), F32)
    slot_of = jnp.zeros((n, LANE), jnp.int32)
    for k in range(SLOTS):
        here = lane_n == lanes_at[:, k:k + 1]
        spread = spread + jnp.where(here, weights[:, k:k + 1], 0.0)
        slot_of = jnp.where(here, SLOTS + k, slot_of)
    pi_row[...] = spread
    k_of[...] = slot_of
    row_id = lax.div(cell_v[0][0:1, :], LANE)
    row_id = jnp.concatenate([row_id] * 3, axis=1)
    grid_rows = lax.broadcasted_iota(jnp.int32, (layers * SUB, 3 * n), 0)
    onehot[...] = jnp.where(grid_rows == row_id, 1.0, 0.0).astype(jnp.bfloat16)
    same[...] = jnp.where(lax.div(places[:, 0:1], LANE) == row_id, 1.0, 0.0).astype(jnp.bfloat16)

    def split(field):
        high = field.astype(jnp.bfloat16)
        rest = field - high.astype(F32)
        mid = rest.astype(jnp.bfloat16)
        low = (rest - mid.astype(F32)).astype(jnp.bfloat16)
        return jnp.concatenate([high, mid, low], axis=0)

    def scatter():
        total = jnp.dot(onehot[...], flow[...], preferred_element_type=F32)
        into[...] = total.reshape(layers, SUB, LANE)

    flow[...] = split(spread)
    scatter()

    zc = 4 if layers % 4 == 0 else 1
    chunks = [slice(z, z + zc) for z in range(0, layers, zc)]
    lane = lax.broadcasted_iota(jnp.int32, (SUB, LANE), 1)
    row = lax.broadcasted_iota(jnp.int32, (SUB, LANE), 0)
    edge = (lane == 0) | (lane == LANE - 1)

    tz[:, 0] = jnp.zeros((3, SUB, LANE), F32)
    tz[:, layers + 1] = jnp.zeros((3, SUB, LANE), F32)

    def flat(zs):
        return slice(zs.start * SUB, zs.stop * SUB)

    def publish(zs, vec, packed):
        mv = apply3([mm[i, zs] for i in range(9)], vec)
        for c in range(3):
            v[c, flat(zs), :] = vec[c].reshape(zc * SUB, LANE)
            tx[c, zs] = tt[0, zs] * mv[c]
            along = tt[1, zs] * mv[c]
            ty[c, zs] = along
            tz[c, zs.start + 1:zs.stop + 1] = tt[2, zs] * mv[c]
            for z in range(zs.start, zs.stop):
                shift = (2 * (c * layers + z)) % LANE
                moved = along[z - zs.start]
                if shift:
                    moved = pltpu.roll(moved, shift, 1)
                mine = (lane == (shift - 1) % LANE) | (lane == shift)
                packed = jnp.where(mine, moved, packed)
        return packed

    for load in loads[4:]:
        load.wait()
    for zs in chunks:
        dense = [diag[i, zs].astype(F32) for i in range(9)]
        mobile = [mob[i, zs].astype(F32) for i in range(9)]
        inv = inverse3(dense)
        perf = into[zs]
        for i in range(9):
            dinv[i, zs] = inv[i]
            mm[i, zs] = mobile[i]
            dd[i, zs] = dense[i] + mobile[i] * perf if i % 3 == 0 else dense[i]
        for i in range(3):
            tt[i, zs] = trans[i, zs].astype(F32)
        ty_edge[zs] = jnp.where(edge, tt[1, zs], 0.0)
        gain = apply3(inv, [mobile[0], mobile[3], mobile[6]])
        vec = apply3(inv, [rhs[c, zs] for c in range(3)])
        for c in range(3):
            kk[c, flat(zs), :] = gain[c].reshape(zc * SUB, LANE)
            v[c, flat(zs), :] = vec[c].reshape(zc * SUB, LANE)
    flow[...] = jnp.zeros_like(flow)

    def pick_rows(source, target):
        for o in range(n):
            at = lax.div(cell_s[0, 0, o], LANE)
            target[o:o + 1, :] = source[0, pl.ds(at, 1), :]

    pick_rows(kk, k_rows)
    pick_rows(v, rows)

    seg[...] = jnp.zeros_like(seg)
    seg[0, 0:seg_rows, :] = jnp.where(parent[...] >= 0, seg_trans[...], 0.0)
    seg[2, 0:seg_rows, :] = seg_trans[...]
    seg[3, 0:seg_rows, :] = seg_rhs[...]

    def before(x):
        moved = pltpu.roll(x, 1, 1)
        return jnp.where(lane == 0, pltpu.roll(moved, 1, 0), moved)

    def after(x):
        moved = pltpu.roll(x, LANE - 1, 1)
        return jnp.where(lane == LANE - 1, pltpu.roll(moved, SUB - 1, 0), moved)

    def tile(parts):
        total = jnp.zeros((SUB, LANE), F32)
        for r in range(seg_rows):
            total = jnp.where(row == r, jnp.sum(parts[r], axis=0, keepdims=True), total)
        return total

    seg[1] = after(seg[0])
    wait_rows(0)
    came = arrived(0)
    parts = [jnp.zeros((n, LANE), F32) for _ in range(seg_rows)]
    for k in range(SLOTS):
        goes = places[:, SLOTS + k:SLOTS + k + 1]
        for r in range(seg_rows):
            term = jnp.where(lane_n + r * LANE == goes, came[:, k:k + 1], 0.0)
            feed[k, r] = term
            parts[r] = parts[r] + term
    turn_i[0:n, :] = lax.div(places, LANE)
    seg[2] = jnp.where(row < seg_rows, seg[2] + seg[1] + tile(parts), 1.0)
    seg[4] = seg[3] / seg[2]
    sums[...] = jnp.zeros_like(sums)

    def fill(slot):
        where_to = idx[...]
        which = turn_i[0:n, :]
        state = seg[4]
        there = rows[...] + k_rows[...] * jnp.dot(
            same[...], flow[...], preferred_element_type=F32)
        row_vals = jnp.take_along_axis(there, where_to, axis=1, mode="promise_in_bounds")
        seg_vals = jnp.zeros((n, LANE), F32)
        for r in range(seg_rows):
            whole = jnp.broadcast_to(state[r:r + 1, :], (n, LANE))
            got = jnp.take_along_axis(whole, where_to, axis=1, mode="promise_in_bounds")
            seg_vals = jnp.where(which == r, got, seg_vals)
        total = jnp.broadcast_to(sums[0:1, :], (n, LANE))
        send[slot] = jnp.where(
            lane_n < SLOTS, row_vals, jnp.where(lane_n < 2 * SLOTS, seg_vals, total))

    def advance(slot):
        scatter()
        packed = jnp.zeros((SUB, LANE), F32)
        for zs in chunks:
            vec = [
                v[c, flat(zs), :].reshape(zc, SUB, LANE)
                + kk[c, flat(zs), :].reshape(zc, SUB, LANE) * into[zs]
                for c in range(3)
            ]
            packed = publish(zs, vec, packed)
        ypack[slot] = packed

    def inside():
        for zs in chunks:
            vec = [v[c, flat(zs), :].reshape(zc, SUB, LANE) for c in range(3)]
            pulled = apply3([dd[i, zs] for i in range(9)], vec)
            for c in range(3):
                x, y = tx[c, zs], ty[c, zs]
                near_x = (
                    jnp.where(row == 0, 0.0, pltpu.roll(x, 1, 1))
                    + jnp.where(row == SUB - 1, 0.0, pltpu.roll(x, SUB - 1, 1)))
                near_y = (
                    jnp.where(lane == 0, 0.0, pltpu.roll(y, 1, 2))
                    + jnp.where(lane == LANE - 1, 0.0, pltpu.roll(y, LANE - 1, 2)))
                near_z = tz[c, zs] + tz[c, zs.start + 2:zs.stop + 2]
                part[c, zs] = (
                    rhs[c, zs] - pulled[c]
                    + (tt[0, zs] * near_x + tt[1, zs] * near_y + tt[2, zs] * near_z))

    def rest():
        g = seg[4]
        return seg[3] - seg[2] * g + seg[0] * before(g) + seg[1] * after(g)

    def fed(came):
        parts = [jnp.zeros((n, LANE), F32) for _ in range(seg_rows)]
        for k in range(SLOTS):
            value = jnp.broadcast_to(came[:, k:k + 1], (n, LANE))
            for r in range(seg_rows):
                parts[r] = parts[r] + value * feed[k, r]
        return tile(parts)

    def receive(slot):
        base = rest()
        wait_rows(slot)
        came = arrived(slot)
        pressure = jnp.take_along_axis(came, k_of[...], axis=1, mode="promise_in_bounds")
        flow[...] = split(pi_row[...] * pressure)
        seg[5] = base + fed(came)
        return came

    def borders(slot, last):
        wait_halos(slot)
        border = jnp.where(
            lax.rem(lane, 2) == 0,
            pltpu.roll(yrecv[slot, 0], 1, 1), pltpu.roll(yrecv[slot, 1], LANE - 1, 1))
        for zs in chunks:
            vec = []
            for c in range(3):
                total = part[c, zs] + tt[0, zs] * xrecv[slot, c, zs]
                sides = []
                for z in range(zs.start, zs.stop):
                    shift = (2 * (c * layers + z)) % LANE
                    sides.append(pltpu.roll(border, LANE - shift, 1) if shift else border)
                total = total + ty_edge[zs] * jnp.stack(sides)
                res[c, zs] = total
                vec.append(total)
            if not last:
                step = apply3([dinv[i, zs] for i in range(9)], vec)
                for c in range(3):
                    v[c, flat(zs), :] = v[c, flat(zs), :] + step[c].reshape(zc * SUB, LANE)

    def put_sums(numer, denom):
        first = jnp.sum(jnp.sum(numer, axis=0, keepdims=True), axis=1, keepdims=True)
        second = jnp.sum(jnp.sum(denom, axis=0, keepdims=True), axis=1, keepdims=True)
        sums[...] = jnp.where(
            lane == 2 * SLOTS, first, jnp.where(lane == 2 * SLOTS + 1, second, 0.0))

    def ratio(came):
        total = jnp.sum(came, axis=0, keepdims=True)
        return total[:, 2 * SLOTS:2 * SLOTS + 1] / total[:, 2 * SLOTS + 1:2 * SLOTS + 2]

    def keep_state():
        for c in range(3):
            for zs in chunks:
                v4[c, zs] = v[c, flat(zs), :].reshape(zc, SUB, LANE)
        seg[6] = seg[4]

    def keep_residual():
        numer = seg[3] * (seg[3] - seg[5])
        denom = (seg[3] - seg[5]) * (seg[3] - seg[5])
        seg[7] = seg[5]
        for c in range(3):
            for zs in chunks:
                last, start = res[c, zs] + mm[3 * c, zs] * into[zs], rhs[c, zs]
                a4[c, zs] = last
                diff = start - last
                numer = numer + jnp.sum(start * diff, axis=0)
                denom = denom + jnp.sum(diff * diff, axis=0)
        put_sums(numer, denom)

    def exchange(k, slot, last):
        fill(slot)
        advance(slot)
        send_halos(slot)
        send_rows(slot)
        pl.when(k == SWEEPS)(keep_state)
        pl.when(k == SWEEPS + 1)(keep_residual)
        inside()
        borders(slot, last)

    def sweep(k, carry):
        slot = lax.rem(k, 2)
        exchange(k, slot, False)
        pick_rows(v, rows)
        came = receive(slot)

        @pl.when(k == SWEEPS + 2)
        def _():
            sums[1:2, :] = jnp.broadcast_to(ratio(came), (1, LANE))

        seg[4] = seg[4] + seg[5] / seg[2]
        return carry

    last = 2 * SWEEPS
    lax.fori_loop(1, last, sweep, 0)
    slot = last % 2
    omega = sums[1:2, :]
    exchange(last, slot, True)
    receive(slot)
    scatter()

    def mix(old, new):
        return old + omega * (new - old)

    start, middle, end = seg[3], seg[7], seg[5]
    first = mix(start, middle)
    diff = first - mix(middle, end)
    numer, denom = first * diff, diff * diff
    for zs in chunks:
        for c in range(3):
            middle = a4[c, zs]
            first = mix(rhs[c, zs], middle)
            diff = first - mix(middle, res[c, zs] + mm[3 * c, zs] * into[zs])
            numer = numer + jnp.sum(first * diff, axis=0)
            denom = denom + jnp.sum(diff * diff, axis=0)
    put_sums(numer, denom)
    send[1] = jnp.broadcast_to(sums[0:1, :], (n, LANE))
    send_rows(1)
    wait_rows(1)
    second = jnp.broadcast_to(ratio(arrived(1)), (1, LANE))

    def combine(middle, end):
        base = omega * middle
        return base + second * (mix(middle, end) - base)

    for c in range(3):
        for zs in chunks:
            out_u[c, zs] = combine(v4[c, zs], v[c, flat(zs), :].reshape(zc, SUB, LANE))
    out_w[...] = combine(seg[6], seg[4])[0:seg_rows, :]


def on_device(
    rhs, diag_block, mobility, trans, perf_cell, perf_pi, perf_seg, seg_parent, seg_trans, seg_rhs
):
    nx, ny = lax.axis_size("gx"), lax.axis_size("gy")
    n = nx * ny
    layers = rhs.shape[1]
    seg_rows = seg_rhs.shape[0] // LANE
    tiles = (seg_rows, LANE)
    cells = (layers, SUB, LANE)
    vmem = pl.BlockSpec(memory_space=pltpu.VMEM)
    far = pl.BlockSpec(memory_space=pltpu.HBM)

    def scratch(*shape, kind=F32):
        return pltpu.VMEM(shape, kind)

    slots = perf_cell.shape
    half, whole = jnp.bfloat16, jnp.int32
    u, w = pl.pallas_call(
        functools.partial(kernel, nx, ny, layers, seg_rows),
        out_shape=[
            jax.ShapeDtypeStruct(rhs.shape, F32), jax.ShapeDtypeStruct(tiles, F32)],
        in_specs=[far] * 10,
        out_specs=[vmem] * 2,
        scratch_shapes=[
            scratch(3, *cells), scratch(9, *cells, kind=half), scratch(9, *cells, kind=half),
            scratch(3, *cells, kind=half), pltpu.SMEM(slots, whole),
            scratch(*slots, kind=whole), scratch(*slots), scratch(*slots, kind=whole),
            scratch(*tiles, kind=whole), scratch(*tiles), scratch(*tiles),
            scratch(3, layers * SUB, LANE), scratch(3, *cells), scratch(3, *cells),
            scratch(3, layers + 2, SUB, LANE), scratch(3, *cells), scratch(3, *cells),
            scratch(3, *cells), scratch(3, *cells), scratch(9, *cells), scratch(9, *cells),
            scratch(9, *cells), scratch(3, layers * SUB, LANE), scratch(3, *cells),
            scratch(*cells), scratch(*cells),
            scratch(layers * SUB, 3 * n, kind=half), scratch(n, 3 * n, kind=half),
            scratch(SLOTS, seg_rows, n, LANE), scratch(n, LANE),
            scratch(n, LANE, kind=whole), scratch(n, LANE, kind=whole),
            scratch(n, LANE), scratch(n, LANE), scratch(3 * n, LANE, kind=half),
            scratch(2, n, LANE), scratch(2, n, LANE),
            scratch(2, SUB, LANE), scratch(2, 2, SUB, LANE), scratch(2, 3, *cells),
            scratch(LANE, LANE, kind=whole), scratch(LANE, LANE),
            scratch(8, SUB, LANE), scratch(SUB, LANE),
            pltpu.SemaphoreType.DMA((2, 4)), pltpu.SemaphoreType.DMA((2, 4)),
            pltpu.SemaphoreType.DMA((2,)), pltpu.SemaphoreType.DMA((2,)),
            pltpu.SemaphoreType.DMA((11,)),
        ],
        compiler_params=pltpu.CompilerParams(
            collective_id=0, has_side_effects=True, vmem_limit_bytes=62 * 1024 * 1024),
        name="sweeps",
    )(
        rhs, diag_block, mobility, trans, perf_cell, perf_pi, perf_seg,
        seg_parent.reshape(tiles), seg_trans.reshape(tiles), seg_rhs.reshape(tiles),
    )
    return u, w.reshape(-1)


def solution(mesh):
    return jax.shard_map(
        on_device,
        mesh=mesh,
        in_specs=(
            P(None, None, "gx", "gy"),
            P(None, None, "gx", "gy"),
            P(None, None, "gx", "gy"),
            P(None, None, "gx", "gy"),
            P(("gx", "gy"), None, None),
            P(("gx", "gy"), None, None),
            P(("gx", "gy"), None, None),
            P(("gx", "gy")),
            P(("gx", "gy")),
            P(("gx", "gy")),
        ),
        out_specs=(P(None, None, "gx", "gy"), P(("gx", "gy"))),
        check_vma=False,
    )
```

```python
import functools

import jax
import jax.numpy as jnp
from jax import lax
from jax.experimental import pallas as pl
from jax.experimental.pallas import tpu as pltpu
from jax.sharding import PartitionSpec as P

SWEEPS = 4
SUB, LANE = 8, 128
SLOTS = 8
MESH = pl.DeviceIdType.MESH
F32 = jnp.float32


def apply3(mat, vec):
    return [mat[3 * r] * vec[0] + mat[3 * r + 1] * vec[1] + mat[3 * r + 2] * vec[2] for r in range(3)]


def inverse3(m):
    a, b, c, d, e, f, g, h, i = m
    first = e * i - f * h
    second = f * g - d * i
    third = d * h - e * g
    inv = 1.0 / (a * first + b * second + c * third)
    entries = [
        first, c * h - b * i, b * f - c * e,
        second, a * i - c * g, c * d - a * f,
        third, b * g - a * h, a * e - b * d,
    ]
    return [entry * inv for entry in entries]


def kernel(
    nx, ny, layers, seg_rows,
    rhs_h, diag_h, mob_h, trans_h, cell_h, pi_h, seg_h, parent_h, seg_trans_h, seg_rhs_h,
    out_u, out_w,
    rhs, diag, mob, trans, cell_s, cell_v, perf_pi, perf_seg, parent, seg_trans, seg_rhs,
    v, tx, ty, tz, part, res, v4, a4, dinv, dd, mm, kk, tt, ty_edge, into,
    onehot, same, feed, pi_row, k_of, idx, rows, k_rows, flow, send, recv, ypack, yrecv, xrecv,
    turn_i, turn_f, seg, sums,
    halo_send, halo_recv, msg_send, msg_recv, load_sem,
):
    n = nx * ny
    my_x, my_y = lax.axis_index("gx"), lax.axis_index("gy")
    me = my_x * ny + my_y
    barrier = pltpu.get_barrier_semaphore()

    loads = [
        pltpu.make_async_copy(src, dst, load_sem.at[i])
        for i, (src, dst) in enumerate([
            (cell_h, cell_v), (pi_h, perf_pi), (seg_h, perf_seg), (cell_h, cell_s),
            (diag_h, diag), (mob_h, mob), (trans_h, trans), (rhs_h, rhs),
            (parent_h, parent), (seg_trans_h, seg_trans), (seg_rhs_h, seg_rhs),
        ])
    ]
    for load in loads:
        load.start()

    at_x = [my_x] + [lax.rem(my_x + a, nx) for a in range(1, nx)]
    at_y = [my_y] + [lax.rem(my_y + b, ny) for b in range(1, ny)]
    far_first = sorted(range(ny), key=lambda b: -min(b, ny - b))
    partners = [(at_x[a], at_y[b]) for b in far_first for a in reversed(range(nx)) if a + b]

    xrecv[...] = jnp.zeros_like(xrecv)
    yrecv[...] = jnp.zeros_like(yrecv)
    for target in partners:
        pl.semaphore_signal(barrier, inc=1, device_id=target, device_id_type=MESH)

    has_x = [my_x > 0, my_x < nx - 1]
    has_y = [my_y > 0, my_y < ny - 1]

    def halos(slot):
        below_x, above_x = lax.max(my_x - 1, 0), lax.min(my_x + 1, nx - 1)
        below_y, above_y = lax.max(my_y - 1, 0), lax.min(my_y + 1, ny - 1)

        def copy(src, dst, way, device):
            return pltpu.make_async_remote_copy(
                src_ref=src, dst_ref=dst, send_sem=halo_send.at[slot, way],
                recv_sem=halo_recv.at[slot, way], device_id=device, device_id_type=MESH,
            )

        return [
            (has_x[1], has_x[0], copy(
                tx.at[:, :, SUB - 1:SUB, :], xrecv.at[slot, :, :, 0:1, :], 0, (above_x, my_y))),
            (has_x[0], has_x[1], copy(
                tx.at[:, :, 0:1, :], xrecv.at[slot, :, :, SUB - 1:SUB, :], 1, (below_x, my_y))),
            (has_y[1], has_y[0], copy(ypack.at[slot], yrecv.at[slot, 0], 2, (my_x, above_y))),
            (has_y[0], has_y[1], copy(ypack.at[slot], yrecv.at[slot, 1], 3, (my_x, below_y))),
        ]

    def send_halos(slot):
        for to, _, copy in halos(slot):
            pl.when(to)(copy.start)

    def wait_halos(slot):
        for to, come, copy in halos(slot):
            pl.when(come)(copy.wait_recv)
            pl.when(to)(copy.wait_send)

    def send_rows(slot):
        for target in partners:
            pos = target[0] * ny + target[1]
            pltpu.make_async_remote_copy(
                src_ref=send.at[slot, pl.ds(pos, 1), :], dst_ref=recv.at[slot, pl.ds(me, 1), :],
                send_sem=msg_send.at[slot], recv_sem=msg_recv.at[slot],
                device_id=target, device_id_type=MESH,
            ).start()

    def wait_rows(slot):
        some = pl.ds(0, n - 1)
        copy = pltpu.make_async_remote_copy(
            src_ref=send.at[slot, some, :], dst_ref=recv.at[slot, some, :],
            send_sem=msg_send.at[slot], recv_sem=msg_recv.at[slot],
            device_id=(my_x, my_y), device_id_type=MESH,
        )
        copy.wait_recv()
        copy.wait_send()

    row_n = lax.broadcasted_iota(jnp.int32, (n, LANE), 0)
    lane_n = lax.broadcasted_iota(jnp.int32, (n, LANE), 1)

    def arrived(slot):
        return jnp.where(row_n == me, send[slot], recv[slot])

    turn_i[...] = jnp.zeros_like(turn_i)
    turn_f[...] = jnp.zeros_like(turn_f)
    for load in loads[:4]:
        load.wait()
    turn_i[0:SLOTS, 0:n] = cell_v[0]
    turn_i[SLOTS:2 * SLOTS, 0:n] = perf_seg[0]
    turn_f[0:SLOTS, 0:n] = perf_pi[0]
    places = turn_i[...].T[0:n, :]
    weights = turn_f[...].T[0:n, :]
    send[0] = weights
    pl.semaphore_wait(barrier, n - 1)
    send_rows(0)

    lanes_at = lax.rem(places, LANE)
    idx[...] = lanes_at
    spread = jnp.zeros((n, LANE), F32)
    slot_of = jnp.zeros((n, LANE), jnp.int32)
    for k in range(SLOTS):
        here = lane_n == lanes_at[:, k:k + 1]
        spread = spread + jnp.where(here, weights[:, k:k + 1], 0.0)
        slot_of = jnp.where(here, SLOTS + k, slot_of)
    pi_row[...] = spread
    k_of[...] = slot_of
    row_id = lax.div(cell_v[0][0:1, :], LANE)
    row_id = jnp.concatenate([row_id] * 3, axis=1)
    grid_rows = lax.broadcasted_iota(jnp.int32, (layers * SUB, 3 * n), 0)
    onehot[...] = jnp.where(grid_rows == row_id, 1.0, 0.0).astype(jnp.bfloat16)
    same[...] = jnp.where(lax.div(places[:, 0:1], LANE) == row_id, 1.0, 0.0).astype(jnp.bfloat16)

    def split(field):
        high = field.astype(jnp.bfloat16)
        rest = field - high.astype(F32)
        mid = rest.astype(jnp.bfloat16)
        low = (rest - mid.astype(F32)).astype(jnp.bfloat16)
        return jnp.concatenate([high, mid, low], axis=0)

    def scatter():
        total = jnp.dot(onehot[...], flow[...], preferred_element_type=F32)
        into[...] = total.reshape(layers, SUB, LANE)

    flow[...] = split(spread)
    scatter()

    zc = 4 if layers % 4 == 0 else 1
    chunks = [slice(z, z + zc) for z in range(0, layers, zc)]
    lane = lax.broadcasted_iota(jnp.int32, (SUB, LANE), 1)
    row = lax.broadcasted_iota(jnp.int32, (SUB, LANE), 0)
    edge = (lane == 0) | (lane == LANE - 1)

    tz[:, 0] = jnp.zeros((3, SUB, LANE), F32)
    tz[:, layers + 1] = jnp.zeros((3, SUB, LANE), F32)

    def flat(zs):
        return slice(zs.start * SUB, zs.stop * SUB)

    def publish(zs, vec, packed):
        mv = apply3([mm[i, zs] for i in range(9)], vec)
        for c in range(3):
            v[c, flat(zs), :] = vec[c].reshape(zc * SUB, LANE)
            tx[c, zs] = tt[0, zs] * mv[c]
            along = tt[1, zs] * mv[c]
            ty[c, zs] = along
            tz[c, zs.start + 1:zs.stop + 1] = tt[2, zs] * mv[c]
            for z in range(zs.start, zs.stop):
                shift = (2 * (c * layers + z)) % LANE
                moved = along[z - zs.start]
                if shift:
                    moved = pltpu.roll(moved, shift, 1)
                mine = (lane == (shift - 1) % LANE) | (lane == shift)
                packed = jnp.where(mine, moved, packed)
        return packed

    for load in loads[4:]:
        load.wait()
    for zs in chunks:
        dense = [diag[i, zs].astype(F32) for i in range(9)]
        mobile = [mob[i, zs].astype(F32) for i in range(9)]
        inv = inverse3(dense)
        perf = into[zs]
        for i in range(9):
            dinv[i, zs] = inv[i]
            mm[i, zs] = mobile[i]
            dd[i, zs] = dense[i] + mobile[i] * perf if i % 3 == 0 else dense[i]
        for i in range(3):
            tt[i, zs] = trans[i, zs].astype(F32)
        ty_edge[zs] = jnp.where(edge, tt[1, zs], 0.0)
        gain = apply3(inv, [mobile[0], mobile[3], mobile[6]])
        vec = apply3(inv, [rhs[c, zs] for c in range(3)])
        for c in range(3):
            kk[c, flat(zs), :] = gain[c].reshape(zc * SUB, LANE)
            v[c, flat(zs), :] = vec[c].reshape(zc * SUB, LANE)
    flow[...] = jnp.zeros_like(flow)

    def pick_rows(source, target):
        tiles = []
        for first in range(0, n, SUB):
            tile = jnp.zeros((SUB, LANE), F32)
            for o in range(SUB):
                at = lax.shift_right_logical(cell_s[0, 0, first + o], LANE.bit_length() - 1)
                one = jnp.broadcast_to(source[0, pl.ds(at, 1), :], (SUB, LANE))
                tile = jnp.where(row == o, one, tile)
            tiles.append(tile)
        for i, tile in enumerate(tiles):
            target[i * SUB:(i + 1) * SUB, :] = tile

    pick_rows(kk, k_rows)
    pick_rows(v, rows)

    seg[...] = jnp.zeros_like(seg)
    seg[0, 0:seg_rows, :] = jnp.where(parent[...] >= 0, seg_trans[...], 0.0)
    seg[2, 0:seg_rows, :] = seg_trans[...]
    seg[3, 0:seg_rows, :] = seg_rhs[...]

    def before(x):
        moved = pltpu.roll(x, 1, 1)
        return jnp.where(lane == 0, pltpu.roll(moved, 1, 0), moved)

    def after(x):
        moved = pltpu.roll(x, LANE - 1, 1)
        return jnp.where(lane == LANE - 1, pltpu.roll(moved, SUB - 1, 0), moved)

    def tile(parts):
        total = jnp.zeros((SUB, LANE), F32)
        for r in range(seg_rows):
            total = jnp.where(row == r, jnp.sum(parts[r], axis=0, keepdims=True), total)
        return total

    seg[1] = after(seg[0])
    wait_rows(0)
    came = arrived(0)
    parts = [jnp.zeros((n, LANE), F32) for _ in range(seg_rows)]
    for k in range(SLOTS):
        goes = places[:, SLOTS + k:SLOTS + k + 1]
        for r in range(seg_rows):
            term = jnp.where(lane_n + r * LANE == goes, came[:, k:k + 1], 0.0)
            feed[k, r] = term
            parts[r] = parts[r] + term
    turn_i[0:n, :] = lax.div(places, LANE)
    seg[2] = jnp.where(row < seg_rows, seg[2] + seg[1] + tile(parts), 1.0)
    seg[4] = seg[3] / seg[2]
    sums[...] = jnp.zeros_like(sums)

    def fill(slot):
        where_to = idx[...]
        which = turn_i[0:n, :]
        state = seg[4]
        there = rows[...] + k_rows[...] * jnp.dot(
            same[...], flow[...], preferred_element_type=F32)
        row_vals = jnp.take_along_axis(there, where_to, axis=1, mode="promise_in_bounds")
        seg_vals = jnp.zeros((n, LANE), F32)
        for r in range(seg_rows):
            whole = jnp.broadcast_to(state[r:r + 1, :], (n, LANE))
            got = jnp.take_along_axis(whole, where_to, axis=1, mode="promise_in_bounds")
            seg_vals = jnp.where(which == r, got, seg_vals)
        total = jnp.broadcast_to(sums[0:1, :], (n, LANE))
        send[slot] = jnp.where(
            lane_n < SLOTS, row_vals, jnp.where(lane_n < 2 * SLOTS, seg_vals, total))

    def advance(slot):
        scatter()
        packed = jnp.zeros((SUB, LANE), F32)
        for zs in chunks:
            vec = [
                v[c, flat(zs), :].reshape(zc, SUB, LANE)
                + kk[c, flat(zs), :].reshape(zc, SUB, LANE) * into[zs]
                for c in range(3)
            ]
            packed = publish(zs, vec, packed)
        ypack[slot] = packed

    def inside():
        for zs in chunks:
            vec = [v[c, flat(zs), :].reshape(zc, SUB, LANE) for c in range(3)]
            pulled = apply3([dd[i, zs] for i in range(9)], vec)
            for c in range(3):
                x, y = tx[c, zs], ty[c, zs]
                near_x = (
                    jnp.where(row == 0, 0.0, pltpu.roll(x, 1, 1))
                    + jnp.where(row == SUB - 1, 0.0, pltpu.roll(x, SUB - 1, 1)))
                near_y = (
                    jnp.where(lane == 0, 0.0, pltpu.roll(y, 1, 2))
                    + jnp.where(lane == LANE - 1, 0.0, pltpu.roll(y, LANE - 1, 2)))
                near_z = tz[c, zs] + tz[c, zs.start + 2:zs.stop + 2]
                part[c, zs] = (
                    rhs[c, zs] - pulled[c]
                    + (tt[0, zs] * near_x + tt[1, zs] * near_y + tt[2, zs] * near_z))

    def rest():
        g = seg[4]
        return seg[3] - seg[2] * g + seg[0] * before(g) + seg[1] * after(g)

    def fed(came):
        parts = [jnp.zeros((n, LANE), F32) for _ in range(seg_rows)]
        for k in range(SLOTS):
            value = jnp.broadcast_to(came[:, k:k + 1], (n, LANE))
            for r in range(seg_rows):
                parts[r] = parts[r] + value * feed[k, r]
        return tile(parts)

    def receive(slot):
        base = rest()
        wait_rows(slot)
        came = arrived(slot)
        pressure = jnp.take_along_axis(came, k_of[...], axis=1, mode="promise_in_bounds")
        flow[...] = split(pi_row[...] * pressure)
        seg[5] = base + fed(came)
        return came

    def borders(slot, last):
        wait_halos(slot)
        border = jnp.where(
            lax.rem(lane, 2) == 0,
            pltpu.roll(yrecv[slot, 0], 1, 1), pltpu.roll(yrecv[slot, 1], LANE - 1, 1))
        for zs in chunks:
            vec = []
            for c in range(3):
                total = part[c, zs] + tt[0, zs] * xrecv[slot, c, zs]
                sides = []
                for z in range(zs.start, zs.stop):
                    shift = (2 * (c * layers + z)) % LANE
                    sides.append(pltpu.roll(border, LANE - shift, 1) if shift else border)
                total = total + ty_edge[zs] * jnp.stack(sides)
                res[c, zs] = total
                vec.append(total)
            if not last:
                step = apply3([dinv[i, zs] for i in range(9)], vec)
                for c in range(3):
                    v[c, flat(zs), :] = v[c, flat(zs), :] + step[c].reshape(zc * SUB, LANE)

    def put_sums(numer, denom):
        first = jnp.sum(jnp.sum(numer, axis=0, keepdims=True), axis=1, keepdims=True)
        second = jnp.sum(jnp.sum(denom, axis=0, keepdims=True), axis=1, keepdims=True)
        sums[...] = jnp.where(
            lane == 2 * SLOTS, first, jnp.where(lane == 2 * SLOTS + 1, second, 0.0))

    def ratio(came):
        total = jnp.sum(came, axis=0, keepdims=True)
        return total[:, 2 * SLOTS:2 * SLOTS + 1] / total[:, 2 * SLOTS + 1:2 * SLOTS + 2]

    def keep_state():
        for c in range(3):
            for zs in chunks:
                v4[c, zs] = v[c, flat(zs), :].reshape(zc, SUB, LANE)
        seg[6] = seg[4]

    def keep_residual():
        numer = seg[3] * (seg[3] - seg[5])
        denom = (seg[3] - seg[5]) * (seg[3] - seg[5])
        seg[7] = seg[5]
        for c in range(3):
            for zs in chunks:
                last, start = res[c, zs] + mm[3 * c, zs] * into[zs], rhs[c, zs]
                a4[c, zs] = last
                diff = start - last
                numer = numer + jnp.sum(start * diff, axis=0)
                denom = denom + jnp.sum(diff * diff, axis=0)
        put_sums(numer, denom)

    def exchange(k, slot, last):
        fill(slot)
        advance(slot)
        send_halos(slot)
        send_rows(slot)
        pl.when(k == SWEEPS)(keep_state)
        pl.when(k == SWEEPS + 1)(keep_residual)
        inside()
        borders(slot, last)

    def sweep(k, slot):
        exchange(k, slot, False)
        pick_rows(v, rows)
        came = receive(slot)

        @pl.when(k == SWEEPS + 2)
        def _():
            sums[1:2, :] = jnp.broadcast_to(ratio(came), (1, LANE))

        seg[4] = seg[4] + seg[5] / seg[2]

    def two_sweeps(pair, carry):
        sweep(2 * pair + 1, 1)
        sweep(2 * pair + 2, 0)
        return carry

    last = 2 * SWEEPS
    lax.fori_loop(0, SWEEPS - 1, two_sweeps, 0)
    sweep(last - 1, 1)
    slot = 0
    omega = sums[1:2, :]
    exchange(last, slot, True)
    receive(slot)
    scatter()

    def mix(old, new):
        return old + omega * (new - old)

    start, middle, end = seg[3], seg[7], seg[5]
    first = mix(start, middle)
    diff = first - mix(middle, end)
    numer, denom = first * diff, diff * diff
    for zs in chunks:
        for c in range(3):
            middle = a4[c, zs]
            first = mix(rhs[c, zs], middle)
            diff = first - mix(middle, res[c, zs] + mm[3 * c, zs] * into[zs])
            numer = numer + jnp.sum(first * diff, axis=0)
            denom = denom + jnp.sum(diff * diff, axis=0)
    put_sums(numer, denom)
    send[1] = jnp.broadcast_to(sums[0:1, :], (n, LANE))
    send_rows(1)
    wait_rows(1)
    second = jnp.broadcast_to(ratio(arrived(1)), (1, LANE))

    def combine(middle, end):
        base = omega * middle
        return base + second * (mix(middle, end) - base)

    for c in range(3):
        for zs in chunks:
            out_u[c, zs] = combine(v4[c, zs], v[c, flat(zs), :].reshape(zc, SUB, LANE))
    out_w[...] = combine(seg[6], seg[4])[0:seg_rows, :]


def on_device(
    rhs, diag_block, mobility, trans, perf_cell, perf_pi, perf_seg, seg_parent, seg_trans, seg_rhs
):
    nx, ny = lax.axis_size("gx"), lax.axis_size("gy")
    n = nx * ny
    layers = rhs.shape[1]
    seg_rows = seg_rhs.shape[0] // LANE
    tiles = (seg_rows, LANE)
    cells = (layers, SUB, LANE)
    vmem = pl.BlockSpec(memory_space=pltpu.VMEM)
    far = pl.BlockSpec(memory_space=pltpu.HBM)

    def scratch(*shape, kind=F32):
        return pltpu.VMEM(shape, kind)

    slots = perf_cell.shape
    half, whole = jnp.bfloat16, jnp.int32
    u, w = pl.pallas_call(
        functools.partial(kernel, nx, ny, layers, seg_rows),
        out_shape=[
            jax.ShapeDtypeStruct(rhs.shape, F32), jax.ShapeDtypeStruct(tiles, F32)],
        in_specs=[far] * 10,
        out_specs=[vmem] * 2,
        scratch_shapes=[
            scratch(3, *cells), scratch(9, *cells, kind=half), scratch(9, *cells, kind=half),
            scratch(3, *cells, kind=half), pltpu.SMEM(slots, whole),
            scratch(*slots, kind=whole), scratch(*slots), scratch(*slots, kind=whole),
            scratch(*tiles, kind=whole), scratch(*tiles), scratch(*tiles),
            scratch(3, layers * SUB, LANE), scratch(3, *cells), scratch(3, *cells),
            scratch(3, layers + 2, SUB, LANE), scratch(3, *cells), scratch(3, *cells),
            scratch(3, *cells), scratch(3, *cells), scratch(9, *cells), scratch(9, *cells),
            scratch(9, *cells), scratch(3, layers * SUB, LANE), scratch(3, *cells),
            scratch(*cells), scratch(*cells),
            scratch(layers * SUB, 3 * n, kind=half), scratch(n, 3 * n, kind=half),
            scratch(SLOTS, seg_rows, n, LANE), scratch(n, LANE),
            scratch(n, LANE, kind=whole), scratch(n, LANE, kind=whole),
            scratch(n, LANE), scratch(n, LANE), scratch(3 * n, LANE, kind=half),
            scratch(2, n, LANE), scratch(2, n, LANE),
            scratch(2, SUB, LANE), scratch(2, 2, SUB, LANE), scratch(2, 3, *cells),
            scratch(LANE, LANE, kind=whole), scratch(LANE, LANE),
            scratch(8, SUB, LANE), scratch(SUB, LANE),
            pltpu.SemaphoreType.DMA((2, 4)), pltpu.SemaphoreType.DMA((2, 4)),
            pltpu.SemaphoreType.DMA((2,)), pltpu.SemaphoreType.DMA((2,)),
            pltpu.SemaphoreType.DMA((11,)),
        ],
        compiler_params=pltpu.CompilerParams(
            collective_id=0, has_side_effects=True, vmem_limit_bytes=62 * 1024 * 1024),
        name="sweeps",
    )(
        rhs, diag_block, mobility, trans, perf_cell, perf_pi, perf_seg,
        seg_parent.reshape(tiles), seg_trans.reshape(tiles), seg_rhs.reshape(tiles),
    )
    return u, w.reshape(-1)


def solution(mesh):
    return jax.shard_map(
        on_device,
        mesh=mesh,
        in_specs=(
            P(None, None, "gx", "gy"),
            P(None, None, "gx", "gy"),
            P(None, None, "gx", "gy"),
            P(None, None, "gx", "gy"),
            P(("gx", "gy"), None, None),
            P(("gx", "gy"), None, None),
            P(("gx", "gy"), None, None),
            P(("gx", "gy")),
            P(("gx", "gy")),
            P(("gx", "gy")),
        ),
        out_specs=(P(None, None, "gx", "gy"), P(("gx", "gy"))),
        check_vma=False,
    )
```

```python
import functools

import jax
import jax.numpy as jnp
from jax import lax
from jax.experimental import pallas as pl
from jax.experimental.pallas import tpu as pltpu
from jax.sharding import PartitionSpec as P

SWEEPS = 4
SUB, LANE = 8, 128
SLOTS = 8
MESH = pl.DeviceIdType.MESH
F32 = jnp.float32


def apply3(mat, vec):
    return [mat[3 * r] * vec[0] + mat[3 * r + 1] * vec[1] + mat[3 * r + 2] * vec[2] for r in range(3)]


def inverse3(m):
    a, b, c, d, e, f, g, h, i = m
    first = e * i - f * h
    second = f * g - d * i
    third = d * h - e * g
    inv = 1.0 / (a * first + b * second + c * third)
    entries = [
        first, c * h - b * i, b * f - c * e,
        second, a * i - c * g, c * d - a * f,
        third, b * g - a * h, a * e - b * d,
    ]
    return [entry * inv for entry in entries]


def kernel(
    nx, ny, layers, seg_rows,
    rhs_h, diag_h, mob_h, trans_h, cell_h, pi_h, seg_h, parent_h, seg_trans_h, seg_rhs_h,
    out_u, out_w,
    rhs, diag, mob, trans, cell_s, cell_v, perf_pi, perf_seg, parent, seg_trans, seg_rhs,
    v, tx, ty, tz, part, res, v4, a4, dinv, dd, mm, kk, tt, ty_edge, into,
    onehot, same, feed, pi_row, k_of, idx, rows, k_rows, flow, send, recv, ypack, yrecv, xrecv,
    turn_i, turn_f, seg, sums,
    halo_send, halo_recv, msg_send, msg_recv, load_sem,
):
    n = nx * ny
    my_x, my_y = lax.axis_index("gx"), lax.axis_index("gy")
    me = my_x * ny + my_y
    barrier = pltpu.get_barrier_semaphore()

    loads = [
        pltpu.make_async_copy(src, dst, load_sem.at[i])
        for i, (src, dst) in enumerate([
            (cell_h, cell_v), (pi_h, perf_pi), (seg_h, perf_seg), (cell_h, cell_s),
            (diag_h, diag), (mob_h, mob), (trans_h, trans), (rhs_h, rhs),
            (parent_h, parent), (seg_trans_h, seg_trans), (seg_rhs_h, seg_rhs),
        ])
    ]
    for load in loads:
        load.start()

    at_x = [my_x] + [lax.rem(my_x + a, nx) for a in range(1, nx)]
    at_y = [my_y] + [lax.rem(my_y + b, ny) for b in range(1, ny)]
    far_first = sorted(range(ny), key=lambda b: -min(b, ny - b))
    partners = [(at_x[a], at_y[b]) for b in far_first for a in reversed(range(nx)) if a + b]

    xrecv[...] = jnp.zeros_like(xrecv)
    yrecv[...] = jnp.zeros_like(yrecv)
    for target in partners:
        pl.semaphore_signal(barrier, inc=1, device_id=target, device_id_type=MESH)

    has_x = [my_x > 0, my_x < nx - 1]
    has_y = [my_y > 0, my_y < ny - 1]

    def halos(slot):
        below_x, above_x = lax.max(my_x - 1, 0), lax.min(my_x + 1, nx - 1)
        below_y, above_y = lax.max(my_y - 1, 0), lax.min(my_y + 1, ny - 1)

        def copy(src, dst, way, device):
            return pltpu.make_async_remote_copy(
                src_ref=src, dst_ref=dst, send_sem=halo_send.at[slot, way],
                recv_sem=halo_recv.at[slot, way], device_id=device, device_id_type=MESH,
            )

        return [
            (has_x[1], has_x[0], copy(
                tx.at[:, :, SUB - 1:SUB, :], xrecv.at[slot, :, :, 0:1, :], 0, (above_x, my_y))),
            (has_x[0], has_x[1], copy(
                tx.at[:, :, 0:1, :], xrecv.at[slot, :, :, SUB - 1:SUB, :], 1, (below_x, my_y))),
            (has_y[1], has_y[0], copy(ypack.at[slot], yrecv.at[slot, 0], 2, (my_x, above_y))),
            (has_y[0], has_y[1], copy(ypack.at[slot], yrecv.at[slot, 1], 3, (my_x, below_y))),
        ]

    def send_halos(slot):
        for to, _, copy in halos(slot):
            pl.when(to)(copy.start)

    def wait_halos(slot):
        for to, come, copy in halos(slot):
            pl.when(come)(copy.wait_recv)
            pl.when(to)(copy.wait_send)

    def send_rows(slot, some=slice(None)):
        for target in partners[some]:
            pos = target[0] * ny + target[1]
            pltpu.make_async_remote_copy(
                src_ref=send.at[slot, pl.ds(pos, 1), :], dst_ref=recv.at[slot, pl.ds(me, 1), :],
                send_sem=msg_send.at[slot], recv_sem=msg_recv.at[slot],
                device_id=target, device_id_type=MESH,
            ).start()

    def wait_rows(slot):
        some = pl.ds(0, n - 1)
        copy = pltpu.make_async_remote_copy(
            src_ref=send.at[slot, some, :], dst_ref=recv.at[slot, some, :],
            send_sem=msg_send.at[slot], recv_sem=msg_recv.at[slot],
            device_id=(my_x, my_y), device_id_type=MESH,
        )
        copy.wait_recv()
        copy.wait_send()

    row_n = lax.broadcasted_iota(jnp.int32, (n, LANE), 0)
    lane_n = lax.broadcasted_iota(jnp.int32, (n, LANE), 1)

    def arrived(slot):
        return jnp.where(row_n == me, send[slot], recv[slot])

    turn_i[...] = jnp.zeros_like(turn_i)
    turn_f[...] = jnp.zeros_like(turn_f)
    for load in loads[:4]:
        load.wait()
    turn_i[0:SLOTS, 0:n] = cell_v[0]
    turn_i[SLOTS:2 * SLOTS, 0:n] = perf_seg[0]
    turn_f[0:SLOTS, 0:n] = perf_pi[0]
    places = turn_i[...].T[0:n, :]
    weights = turn_f[...].T[0:n, :]
    send[0] = weights
    pl.semaphore_wait(barrier, n - 1)
    send_rows(0)

    lanes_at = lax.rem(places, LANE)
    idx[...] = lanes_at
    spread = jnp.zeros((n, LANE), F32)
    slot_of = jnp.zeros((n, LANE), jnp.int32)
    for k in range(SLOTS):
        here = lane_n == lanes_at[:, k:k + 1]
        spread = spread + jnp.where(here, weights[:, k:k + 1], 0.0)
        slot_of = jnp.where(here, SLOTS + k, slot_of)
    pi_row[...] = spread
    k_of[...] = slot_of
    row_id = lax.div(cell_v[0][0:1, :], LANE)
    row_id = jnp.concatenate([row_id] * 3, axis=1)
    grid_rows = lax.broadcasted_iota(jnp.int32, (layers * SUB, 3 * n), 0)
    onehot[...] = jnp.where(grid_rows == row_id, 1.0, 0.0).astype(jnp.bfloat16)
    same[...] = jnp.where(lax.div(places[:, 0:1], LANE) == row_id, 1.0, 0.0).astype(jnp.bfloat16)

    def split(field):
        high = field.astype(jnp.bfloat16)
        rest = field - high.astype(F32)
        mid = rest.astype(jnp.bfloat16)
        low = (rest - mid.astype(F32)).astype(jnp.bfloat16)
        return jnp.concatenate([high, mid, low], axis=0)

    def scatter():
        total = jnp.dot(onehot[...], flow[...], preferred_element_type=F32)
        into[...] = total.reshape(layers, SUB, LANE)

    flow[...] = split(spread)
    scatter()

    zc = 4 if layers % 4 == 0 else 1
    chunks = [slice(z, z + zc) for z in range(0, layers, zc)]
    few = n // (2 * len(chunks))
    lane = lax.broadcasted_iota(jnp.int32, (SUB, LANE), 1)
    row = lax.broadcasted_iota(jnp.int32, (SUB, LANE), 0)
    edge = (lane == 0) | (lane == LANE - 1)

    tz[:, 0] = jnp.zeros((3, SUB, LANE), F32)
    tz[:, layers + 1] = jnp.zeros((3, SUB, LANE), F32)

    def flat(zs):
        return slice(zs.start * SUB, zs.stop * SUB)

    def publish(zs, vec, packed):
        mv = apply3([mm[i, zs] for i in range(9)], vec)
        for c in range(3):
            v[c, flat(zs), :] = vec[c].reshape(zc * SUB, LANE)
            tx[c, zs] = tt[0, zs] * mv[c]
            along = tt[1, zs] * mv[c]
            ty[c, zs] = along
            tz[c, zs.start + 1:zs.stop + 1] = tt[2, zs] * mv[c]
            for z in range(zs.start, zs.stop):
                shift = (2 * (c * layers + z)) % LANE
                moved = along[z - zs.start]
                if shift:
                    moved = pltpu.roll(moved, shift, 1)
                mine = (lane == (shift - 1) % LANE) | (lane == shift)
                packed = jnp.where(mine, moved, packed)
        return packed

    for load in loads[4:]:
        load.wait()
    for zs in chunks:
        dense = [diag[i, zs].astype(F32) for i in range(9)]
        mobile = [mob[i, zs].astype(F32) for i in range(9)]
        inv = inverse3(dense)
        perf = into[zs]
        for i in range(9):
            dinv[i, zs] = inv[i]
            mm[i, zs] = mobile[i]
            dd[i, zs] = dense[i] + mobile[i] * perf if i % 3 == 0 else dense[i]
        for i in range(3):
            tt[i, zs] = trans[i, zs].astype(F32)
        ty_edge[zs] = jnp.where(edge, tt[1, zs], 0.0)
        gain = apply3(inv, [mobile[0], mobile[3], mobile[6]])
        vec = apply3(inv, [rhs[c, zs] for c in range(3)])
        for c in range(3):
            kk[c, flat(zs), :] = gain[c].reshape(zc * SUB, LANE)
            v[c, flat(zs), :] = vec[c].reshape(zc * SUB, LANE)
    flow[...] = jnp.zeros_like(flow)

    def pick_rows(source, target):
        tiles = []
        for first in range(0, n, SUB):
            tile = jnp.zeros((SUB, LANE), F32)
            for o in range(SUB):
                at = lax.shift_right_logical(cell_s[0, 0, first + o], LANE.bit_length() - 1)
                one = jnp.broadcast_to(source[0, pl.ds(at, 1), :], (SUB, LANE))
                tile = jnp.where(row == o, one, tile)
            tiles.append(tile)
        for i, tile in enumerate(tiles):
            target[i * SUB:(i + 1) * SUB, :] = tile

    pick_rows(kk, k_rows)
    pick_rows(v, rows)

    seg[...] = jnp.zeros_like(seg)
    seg[0, 0:seg_rows, :] = jnp.where(parent[...] >= 0, seg_trans[...], 0.0)
    seg[2, 0:seg_rows, :] = seg_trans[...]
    seg[3, 0:seg_rows, :] = seg_rhs[...]

    def before(x):
        moved = pltpu.roll(x, 1, 1)
        return jnp.where(lane == 0, pltpu.roll(moved, 1, 0), moved)

    def after(x):
        moved = pltpu.roll(x, LANE - 1, 1)
        return jnp.where(lane == LANE - 1, pltpu.roll(moved, SUB - 1, 0), moved)

    def tile(parts):
        total = jnp.zeros((SUB, LANE), F32)
        for r in range(seg_rows):
            total = jnp.where(row == r, jnp.sum(parts[r], axis=0, keepdims=True), total)
        return total

    seg[1] = after(seg[0])
    wait_rows(0)
    came = arrived(0)
    parts = [jnp.zeros((n, LANE), F32) for _ in range(seg_rows)]
    for k in range(SLOTS):
        goes = places[:, SLOTS + k:SLOTS + k + 1]
        for r in range(seg_rows):
            term = jnp.where(lane_n + r * LANE == goes, came[:, k:k + 1], 0.0)
            feed[k, r] = term
            parts[r] = parts[r] + term
    turn_i[0:n, :] = lax.div(places, LANE)
    seg[2] = jnp.where(row < seg_rows, seg[2] + seg[1] + tile(parts), 1.0)
    seg[4] = seg[3] / seg[2]
    sums[...] = jnp.zeros_like(sums)

    def fill(slot):
        where_to = idx[...]
        which = turn_i[0:n, :]
        state = seg[4]
        there = rows[...] + k_rows[...] * jnp.dot(
            same[...], flow[...], preferred_element_type=F32)
        row_vals = jnp.take_along_axis(there, where_to, axis=1, mode="promise_in_bounds")
        seg_vals = jnp.zeros((n, LANE), F32)
        for r in range(seg_rows):
            whole = jnp.broadcast_to(state[r:r + 1, :], (n, LANE))
            got = jnp.take_along_axis(whole, where_to, axis=1, mode="promise_in_bounds")
            seg_vals = jnp.where(which == r, got, seg_vals)
        total = jnp.broadcast_to(sums[0:1, :], (n, LANE))
        send[slot] = jnp.where(
            lane_n < SLOTS, row_vals, jnp.where(lane_n < 2 * SLOTS, seg_vals, total))

    def advance(slot):
        scatter()
        packed = jnp.zeros((SUB, LANE), F32)
        for zs in chunks:
            vec = [
                v[c, flat(zs), :].reshape(zc, SUB, LANE)
                + kk[c, flat(zs), :].reshape(zc, SUB, LANE) * into[zs]
                for c in range(3)
            ]
            packed = publish(zs, vec, packed)
            send_rows(slot, slice(zs.start // zc * few, (zs.start // zc + 1) * few))
        ypack[slot] = packed

    def inside():
        for zs in chunks:
            vec = [v[c, flat(zs), :].reshape(zc, SUB, LANE) for c in range(3)]
            pulled = apply3([dd[i, zs] for i in range(9)], vec)
            for c in range(3):
                x, y = tx[c, zs], ty[c, zs]
                near_x = (
                    jnp.where(row == 0, 0.0, pltpu.roll(x, 1, 1))
                    + jnp.where(row == SUB - 1, 0.0, pltpu.roll(x, SUB - 1, 1)))
                near_y = (
                    jnp.where(lane == 0, 0.0, pltpu.roll(y, 1, 2))
                    + jnp.where(lane == LANE - 1, 0.0, pltpu.roll(y, LANE - 1, 2)))
                near_z = tz[c, zs] + tz[c, zs.start + 2:zs.stop + 2]
                part[c, zs] = (
                    rhs[c, zs] - pulled[c]
                    + (tt[0, zs] * near_x + tt[1, zs] * near_y + tt[2, zs] * near_z))

    def rest():
        g = seg[4]
        return seg[3] - seg[2] * g + seg[0] * before(g) + seg[1] * after(g)

    def fed(came):
        parts = [jnp.zeros((n, LANE), F32) for _ in range(seg_rows)]
        for k in range(SLOTS):
            value = jnp.broadcast_to(came[:, k:k + 1], (n, LANE))
            for r in range(seg_rows):
                parts[r] = parts[r] + value * feed[k, r]
        return tile(parts)

    def receive(slot):
        base = rest()
        wait_rows(slot)
        came = arrived(slot)
        pressure = jnp.take_along_axis(came, k_of[...], axis=1, mode="promise_in_bounds")
        flow[...] = split(pi_row[...] * pressure)
        seg[5] = base + fed(came)
        return came

    def borders(slot, last):
        wait_halos(slot)
        border = jnp.where(
            lax.rem(lane, 2) == 0,
            pltpu.roll(yrecv[slot, 0], 1, 1), pltpu.roll(yrecv[slot, 1], LANE - 1, 1))
        for zs in chunks:
            vec = []
            for c in range(3):
                total = part[c, zs] + tt[0, zs] * xrecv[slot, c, zs]
                sides = []
                for z in range(zs.start, zs.stop):
                    shift = (2 * (c * layers + z)) % LANE
                    sides.append(pltpu.roll(border, LANE - shift, 1) if shift else border)
                total = total + ty_edge[zs] * jnp.stack(sides)
                res[c, zs] = total
                vec.append(total)
            if not last:
                step = apply3([dinv[i, zs] for i in range(9)], vec)
                for c in range(3):
                    v[c, flat(zs), :] = v[c, flat(zs), :] + step[c].reshape(zc * SUB, LANE)

    def put_sums(numer, denom):
        first = jnp.sum(jnp.sum(numer, axis=0, keepdims=True), axis=1, keepdims=True)
        second = jnp.sum(jnp.sum(denom, axis=0, keepdims=True), axis=1, keepdims=True)
        sums[...] = jnp.where(
            lane == 2 * SLOTS, first, jnp.where(lane == 2 * SLOTS + 1, second, 0.0))

    def ratio(came):
        total = jnp.sum(came, axis=0, keepdims=True)
        return total[:, 2 * SLOTS:2 * SLOTS + 1] / total[:, 2 * SLOTS + 1:2 * SLOTS + 2]

    def keep_state():
        for c in range(3):
            for zs in chunks:
                v4[c, zs] = v[c, flat(zs), :].reshape(zc, SUB, LANE)
        seg[6] = seg[4]

    def keep_residual():
        numer = seg[3] * (seg[3] - seg[5])
        denom = (seg[3] - seg[5]) * (seg[3] - seg[5])
        seg[7] = seg[5]
        for c in range(3):
            for zs in chunks:
                last, start = res[c, zs] + mm[3 * c, zs] * into[zs], rhs[c, zs]
                a4[c, zs] = last
                diff = start - last
                numer = numer + jnp.sum(start * diff, axis=0)
                denom = denom + jnp.sum(diff * diff, axis=0)
        put_sums(numer, denom)

    def exchange(k, slot, last):
        fill(slot)
        advance(slot)
        send_halos(slot)
        send_rows(slot, slice(len(chunks) * few, None))
        pl.when(k == SWEEPS)(keep_state)
        pl.when(k == SWEEPS + 1)(keep_residual)
        inside()
        borders(slot, last)

    def sweep(k, slot):
        exchange(k, slot, False)
        pick_rows(v, rows)
        came = receive(slot)

        @pl.when(k == SWEEPS + 2)
        def _():
            sums[1:2, :] = jnp.broadcast_to(ratio(came), (1, LANE))

        seg[4] = seg[4] + seg[5] / seg[2]

    def two_sweeps(pair, carry):
        sweep(2 * pair + 1, 1)
        sweep(2 * pair + 2, 0)
        return carry

    last = 2 * SWEEPS
    lax.fori_loop(0, SWEEPS - 1, two_sweeps, 0)
    sweep(last - 1, 1)
    slot = 0
    omega = sums[1:2, :]
    exchange(last, slot, True)
    receive(slot)
    scatter()

    def mix(old, new):
        return old + omega * (new - old)

    start, middle, end = seg[3], seg[7], seg[5]
    first = mix(start, middle)
    diff = first - mix(middle, end)
    numer, denom = first * diff, diff * diff
    for zs in chunks:
        for c in range(3):
            middle = a4[c, zs]
            first = mix(rhs[c, zs], middle)
            diff = first - mix(middle, res[c, zs] + mm[3 * c, zs] * into[zs])
            numer = numer + jnp.sum(first * diff, axis=0)
            denom = denom + jnp.sum(diff * diff, axis=0)
    put_sums(numer, denom)
    send[1] = jnp.broadcast_to(sums[0:1, :], (n, LANE))
    send_rows(1)
    wait_rows(1)
    second = jnp.broadcast_to(ratio(arrived(1)), (1, LANE))

    def combine(middle, end):
        base = omega * middle
        return base + second * (mix(middle, end) - base)

    for c in range(3):
        for zs in chunks:
            out_u[c, zs] = combine(v4[c, zs], v[c, flat(zs), :].reshape(zc, SUB, LANE))
    out_w[...] = combine(seg[6], seg[4])[0:seg_rows, :]


def on_device(
    rhs, diag_block, mobility, trans, perf_cell, perf_pi, perf_seg, seg_parent, seg_trans, seg_rhs
):
    nx, ny = lax.axis_size("gx"), lax.axis_size("gy")
    n = nx * ny
    layers = rhs.shape[1]
    seg_rows = seg_rhs.shape[0] // LANE
    tiles = (seg_rows, LANE)
    cells = (layers, SUB, LANE)
    vmem = pl.BlockSpec(memory_space=pltpu.VMEM)
    far = pl.BlockSpec(memory_space=pltpu.HBM)

    def scratch(*shape, kind=F32):
        return pltpu.VMEM(shape, kind)

    slots = perf_cell.shape
    half, whole = jnp.bfloat16, jnp.int32
    u, w = pl.pallas_call(
        functools.partial(kernel, nx, ny, layers, seg_rows),
        out_shape=[
            jax.ShapeDtypeStruct(rhs.shape, F32), jax.ShapeDtypeStruct(tiles, F32)],
        in_specs=[far] * 10,
        out_specs=[vmem] * 2,
        scratch_shapes=[
            scratch(3, *cells), scratch(9, *cells, kind=half), scratch(9, *cells, kind=half),
            scratch(3, *cells, kind=half), pltpu.SMEM(slots, whole),
            scratch(*slots, kind=whole), scratch(*slots), scratch(*slots, kind=whole),
            scratch(*tiles, kind=whole), scratch(*tiles), scratch(*tiles),
            scratch(3, layers * SUB, LANE), scratch(3, *cells), scratch(3, *cells),
            scratch(3, layers + 2, SUB, LANE), scratch(3, *cells), scratch(3, *cells),
            scratch(3, *cells), scratch(3, *cells), scratch(9, *cells), scratch(9, *cells),
            scratch(9, *cells), scratch(3, layers * SUB, LANE), scratch(3, *cells),
            scratch(*cells), scratch(*cells),
            scratch(layers * SUB, 3 * n, kind=half), scratch(n, 3 * n, kind=half),
            scratch(SLOTS, seg_rows, n, LANE), scratch(n, LANE),
            scratch(n, LANE, kind=whole), scratch(n, LANE, kind=whole),
            scratch(n, LANE), scratch(n, LANE), scratch(3 * n, LANE, kind=half),
            scratch(2, n, LANE), scratch(2, n, LANE),
            scratch(2, SUB, LANE), scratch(2, 2, SUB, LANE), scratch(2, 3, *cells),
            scratch(LANE, LANE, kind=whole), scratch(LANE, LANE),
            scratch(8, SUB, LANE), scratch(SUB, LANE),
            pltpu.SemaphoreType.DMA((2, 4)), pltpu.SemaphoreType.DMA((2, 4)),
            pltpu.SemaphoreType.DMA((2,)), pltpu.SemaphoreType.DMA((2,)),
            pltpu.SemaphoreType.DMA((11,)),
        ],
        compiler_params=pltpu.CompilerParams(
            collective_id=0, has_side_effects=True, vmem_limit_bytes=62 * 1024 * 1024),
        name="sweeps",
    )(
        rhs, diag_block, mobility, trans, perf_cell, perf_pi, perf_seg,
        seg_parent.reshape(tiles), seg_trans.reshape(tiles), seg_rhs.reshape(tiles),
    )
    return u, w.reshape(-1)


def solution(mesh):
    return jax.shard_map(
        on_device,
        mesh=mesh,
        in_specs=(
            P(None, None, "gx", "gy"),
            P(None, None, "gx", "gy"),
            P(None, None, "gx", "gy"),
            P(None, None, "gx", "gy"),
            P(("gx", "gy"), None, None),
            P(("gx", "gy"), None, None),
            P(("gx", "gy"), None, None),
            P(("gx", "gy")),
            P(("gx", "gy")),
            P(("gx", "gy")),
        ),
        out_specs=(P(None, None, "gx", "gy"), P(("gx", "gy"))),
        check_vma=False,
    )
```
